256 devices in a mesh: dom: 64 (over z, x, core), sub: 4 (over y).
Axes of the slice: x: 4, y: 4, z: 8, core: 2. Of those that a mesh axis runs over, the one named last changes fastest.
Arguments:
- unknowns: float32 [9, 35, 65536], P(None, None, ('dom', 'sub')), may hold values from -6 to 6
- gradients: float32 [3, 3, 65536], P(None, None, ('dom', 'sub')), may hold values from -0.3 to 0.3
- face_normals: float32 [4, 3, 65536], P(None, None, ('dom', 'sub')), may hold values from -0.3 to 0.3
- materials: float32 [3, 65536], P(None, ('dom', 'sub')), may hold values from 0.5 to 2
- live_count: int32 [256], P(('dom', 'sub')), may hold values from 64 to 256, as said below
- neighbour_code: int32 [4, 65536], P(None, ('dom', 'sub')), may hold values from 0 to 1279, as said below
- orientation: int32 [4, 65536], P(None, ('dom', 'sub')), may hold values from 0 to 2
- send_face: int32 [57344], P(('dom', 'sub')), may hold values from 0 to 1023, as said below
- fault_face: int32 [8192], P(('dom', 'sub')), may hold values from 0 to 1023, as said below
- fault_dip: float32 [2, 8192], P(None, ('dom', 'sub')), may hold values from -3.140625 to 3.140625
- cohesion: float32 [15, 8192], P(None, ('dom', 'sub')), may hold values from 0.05 to 1
- stiffness: float32 [3, 35, 35], replicated, may hold values from -1 to 1
- projection: float32 [4, 35, 15], replicated, may hold values from -1 to 1
- lifting: float32 [4, 15, 35], replicated, may hold values from -0.75 to 0.75
- rotations: float32 [3, 15, 15], replicated, may hold values from -1.5 to 1.5
Outputs:
- unknowns_out: float32 [9, 35, 65536], P(None, None, ('dom', 'sub'))
- fault_slip: float32 [3, 15, 8192], P(None, None, ('dom', 'sub'))
The draws below stay inside these ranges and needn't reach their ends.
Inputs may be any that keep to these rules, and one draw needn't show every extreme that they name: A device's cluster elements are its first live_count slots. A device and the device 64 / 2 further along dom with the same sub index hold at most 320 live elements together; some such pair holds exactly that. `neighbour_code`: values below 1024 name face i' of the device's own element e' as i' * 256 + e'; 1024 + k * 28 + s names slot s of halo block k; 1248 + f names fault slot f. Faces of live elements name only faces of live elements; each halo slot that arrives is named by exactly one face, and fault slot f by the face fault_face[f] alone. `send_face`: on each device, block k of 8 holds 28 codes i * 256 + e of faces of live elements, sent to the device o_k further along dom, o = (1, 2, 3, 4, -1, -2, -3, -4). `fault_face`: on each device, 32 distinct codes i * 256 + e of faces of live elements; slot f faces slot f of the device whose sub index differs in its lowest bit.
All inputs are finite; a program needn't handle non-finite values.
Results may differ from the reference program's by a relative error of at most 0.0003.
Values sent between devices are 32-bit elements; how exact they have to be, the bound alone decides.
A program may use at most 128 MiB of HBM per device.

```python
import math
import jax
import jax.numpy as jnp
from jax import lax

E_CAP = 256
SLOT = 28
F_DEV = 32
BASIS = 35
QUANT = 9
FACE_PTS = 15
ORDER = 5
STEPS = 2
E_ALL = 65536
F_ALL = 8192
N_DOM = 64
N_SUB = 4


OFFSETS = (1, 2, 3, 4, -1, -2, -3, -4)


def topology(key):
    devices = N_DOM * N_SUB
    keys = jax.random.split(key, 6)
    half_dom = N_DOM // 2
    base_count = jax.random.randint(keys[0], (N_DOM, N_SUB), E_CAP // 4, E_CAP // 2 + 1)
    heavy = jax.random.randint(keys[1], (half_dom, N_SUB), 0, 8) == 0
    forced = jax.random.randint(keys[2], (), 0, half_dom * N_SUB)
    heavy = heavy | (jnp.arange(half_dom * N_SUB).reshape(half_dom, N_SUB) == forced)
    heavy_side = jax.random.randint(keys[3], (half_dom, N_SUB), 0, 2)
    lower_half = jnp.where(heavy, jnp.where(heavy_side == 0, E_CAP, E_CAP // 4), base_count[:half_dom])
    upper_half = jnp.where(heavy, jnp.where(heavy_side == 0, E_CAP // 4, E_CAP), base_count[half_dom:])
    counts = jnp.concatenate([lower_half, upper_half], axis=0).reshape(devices).astype(jnp.int32)
    face_keys = jax.random.split(keys[4], devices)
    halo_total = 8 * SLOT
    dom_index = (jnp.arange(devices) // N_SUB).astype(jnp.int32)
    offset_table = jnp.array(OFFSETS, jnp.int32)

    def per_device(device_key, count, dom_pos):
        sub_keys = jax.random.split(device_key, 7)
        codes = jnp.arange(4 * E_CAP, dtype=jnp.int32)
        ranking = jax.random.permutation(sub_keys[0], 4 * E_CAP).astype(jnp.int32)
        score = ranking + 4 * E_CAP * (codes % E_CAP >= count).astype(jnp.int32)
        score = jnp.where(codes == 0, -2, score)
        score = jnp.where(codes == 3 * E_CAP + count - 1, -1, score)
        special = jnp.argsort(score, stable=True)[:halo_total + F_DEV].astype(jnp.int32)
        local_code = jax.random.randint(sub_keys[1], (4 * E_CAP,), 0, 4) * E_CAP
        local_code = (local_code + jax.random.randint(sub_keys[2], (4 * E_CAP,), 0, count)).astype(jnp.int32)
        slots = jnp.arange(halo_total, dtype=jnp.int32)
        source_dom = dom_pos - offset_table[slots // SLOT]
        arrives = (source_dom >= 0) & (source_dom < N_DOM)
        fault_faces = special[:F_DEV]
        halo_faces = special[F_DEV:]
        local_code = local_code.at[halo_faces].set(jnp.where(arrives, 4 * E_CAP + slots, local_code[halo_faces]))
        local_code = local_code.at[fault_faces].set(4 * E_CAP + halo_total + jnp.arange(F_DEV, dtype=jnp.int32))
        send_codes = jax.random.randint(sub_keys[3], (halo_total,), 0, 4) * E_CAP
        send_codes = (send_codes + jax.random.randint(sub_keys[4], (halo_total,), 0, count)).astype(jnp.int32)
        chosen = jax.random.randint(sub_keys[5], (), 0, halo_total)
        send_codes = send_codes.at[chosen].set(3 * E_CAP + count - 1)
        send_codes = send_codes.at[(chosen + 1) % halo_total].set(0)
        return (local_code, send_codes, fault_faces)
    neighbour, send_codes, fault_faces = jax.vmap(per_device)(face_keys, counts, dom_index)
    return (counts, neighbour, send_codes, fault_faces)


def draw_live_count(key, part):
    shared = topology(key)
    return shared[0]


def draw_neighbour_code(key, part):
    shared = topology(key)
    devices = N_DOM * N_SUB
    return jnp.transpose(shared[1].reshape(devices, 4, E_CAP), (1, 0, 2)).reshape(4, devices * E_CAP)


def draw_send_face(key, part):
    shared = topology(key)
    return shared[2].reshape(-1)


def draw_fault_face(key, part):
    shared = topology(key)
    return shared[3].reshape(-1)


def plant(entries, stream_key, least, largest):
    dims = entries.shape
    spot = [jax.random.randint(jax.random.fold_in(stream_key, axis), (), 0, dims[axis]) for axis in range(len(dims))]
    entries = entries.at[tuple(spot)].set(least)
    longest = dims.index(max(dims))
    spot[longest] = (spot[longest] + 1) % dims[longest]
    return entries.at[tuple(spot)].set(largest)


def shard_levels(own_key, dims, pieces, smallest, high):
    gain = 1.0
    for axis_at, parts in pieces:
        steps = jax.random.uniform(jax.random.fold_in(jax.random.fold_in(own_key, 6), axis_at), (parts,), jnp.float32, smallest / len(pieces), high / len(pieces))
        gain = gain * jnp.repeat(jnp.exp(steps), dims[axis_at] // parts).reshape((-1,) + (1,) * (len(dims) - 1 - axis_at))
    return gain


def bell_draw(rng, shape, scale, reach, cuts=(), held_as=jnp.bfloat16):
    factor_of = shard_levels(rng, shape, cuts, -0.22, 0.18) if cuts else 1.0
    result = jax.random.normal(rng, shape, jnp.float32) * scale * factor_of
    return jnp.minimum(jnp.maximum(result, -reach), reach).astype(held_as)


def setup_inputs(seed: int = 0) -> dict:
    streams_of = jax.random.split(jax.random.key(seed), 16)
    unknowns = bell_draw(streams_of[0], (QUANT, BASIS, E_ALL), 1.0, 6.0, ((2, 256),), jnp.float32)
    gradients = jnp.clip(jax.random.uniform(streams_of[1], (3, 3, E_ALL), jnp.float32, -0.3, 0.3) * shard_levels(streams_of[1], (3, 3, E_ALL), ((2, 256),), -0.4, 0.0), -0.3, 0.3)
    face_normals = jnp.clip(jax.random.uniform(streams_of[2], (4, 3, E_ALL), jnp.float32, -0.3, 0.3) * shard_levels(streams_of[2], (4, 3, E_ALL), ((2, 256),), -0.4, 0.0), -0.3, 0.3)
    materials = jnp.clip(jnp.exp(math.log(2.0) - 1.3862944 * jax.random.uniform(streams_of[3], (3, E_ALL), jnp.float32) ** shard_levels(streams_of[3], (3, E_ALL), ((1, 256),), -0.2, 0.2)), 0.5, 2.0)
    live_count = draw_live_count(jax.random.fold_in(streams_of[15], 71), 0)
    neighbour_code = draw_neighbour_code(jax.random.fold_in(streams_of[15], 71), 0)
    orientation = plant(jax.random.randint(streams_of[6], (4, E_ALL), 0, 3), jax.random.fold_in(streams_of[6], 1), 0, 2).astype(jnp.int32)
    send_face = draw_send_face(jax.random.fold_in(streams_of[15], 71), 0)
    fault_face = draw_fault_face(jax.random.fold_in(streams_of[15], 71), 0)
    fault_dip = jnp.clip(jax.random.uniform(streams_of[9], (2, F_ALL), jnp.float32, -3.140625, 3.140625), -3.140625, 3.140625)
    cohesion = jnp.clip(jnp.exp(math.log(1.0) - 2.9957323 * jax.random.uniform(streams_of[10], (FACE_PTS, F_ALL), jnp.float32) ** shard_levels(streams_of[10], (FACE_PTS, F_ALL), ((1, 256),), -0.2, 0.2)), 0.05, 1.0)
    stiffness = bell_draw(streams_of[11], (3, BASIS, BASIS), BASIS ** -0.5, 1.0, (), jnp.float32)
    projection = bell_draw(streams_of[12], (4, BASIS, FACE_PTS), BASIS ** -0.5, 1.0, (), jnp.float32)
    lifting = bell_draw(streams_of[13], (4, FACE_PTS, BASIS), (4 * FACE_PTS) ** -0.5, 0.75, (), jnp.float32)
    rotations = bell_draw(streams_of[14], (3, FACE_PTS, FACE_PTS), FACE_PTS ** -0.5, 1.5, (), jnp.float32)
    return {"unknowns": unknowns, "gradients": gradients, "face_normals": face_normals, "materials": materials, "live_count": live_count, "neighbour_code": neighbour_code, "orientation": orientation, "send_face": send_face, "fault_face": fault_face, "fault_dip": fault_dip, "cohesion": cohesion, "stiffness": stiffness, "projection": projection, "lifting": lifting, "rotations": rotations}


OFFSETS = (1, 2, 3, 4, -1, -2, -3, -4)
FRICTION = 0.6
HIGHEST = lax.Precision.HIGHEST

def traction(fields, normal):
    return (fields[0] * normal[0] + fields[3] * normal[1] + fields[5] * normal[2], fields[3] * normal[0] + fields[1] * normal[1] + fields[4] * normal[2], fields[5] * normal[0] + fields[4] * normal[1] + fields[2] * normal[2])

def elastic(fields, normal, materials):
    first_lame, shear_mod, density = (materials[0], materials[1], materials[2])
    normal_speed = fields[6] * normal[0] + fields[7] * normal[1] + fields[8] * normal[2]
    force_x, force_y, force_z = traction(fields, normal)
    pressure = first_lame * normal_speed
    double_mu = 2.0 * shear_mod
    return jnp.stack([-(pressure + double_mu * fields[6] * normal[0]), -(pressure + double_mu * fields[7] * normal[1]), -(pressure + double_mu * fields[8] * normal[2]), -shear_mod * (fields[6] * normal[1] + fields[7] * normal[0]), -shear_mod * (fields[7] * normal[2] + fields[8] * normal[1]), -shear_mod * (fields[6] * normal[2] + fields[8] * normal[0]), -force_x / density, -force_y / density, -force_z / density])

def predict(unknowns, gradients, materials, stiffness):
    current = unknowns
    integrated = unknowns
    factor = 1.0
    for degree in range(1, ORDER):
        following = jnp.zeros_like(unknowns)
        for direction in range(3):
            reshaped = jnp.einsum('qbe,bc->qce', current, stiffness[direction], precision=HIGHEST)
            following = following + elastic(reshaped, gradients[direction], materials)
        current = following
        factor = factor / (degree + 1)
        integrated = integrated + factor * current
    return integrated

def volume(integrated, gradients, materials, stiffness):
    volume_sum = jnp.zeros_like(integrated)
    for direction in range(3):
        applied = elastic(integrated, gradients[direction], materials)
        volume_sum = volume_sum + jnp.einsum('qbe,cb->qce', applied, stiffness[direction], precision=HIGHEST)
    return volume_sum

def face_traces(integrated, projection):
    traces = jnp.einsum('qbe,jbp->qpje', integrated, projection, precision=HIGHEST)
    return traces.reshape(traces.shape[0], traces.shape[1], 4 * integrated.shape[2])

def finish(unknowns, volume_term, own_table, extended, neighbour_code, orientation, face_normals, materials, fault_face, fault_dip, cohesion, live_rows, lifting, rotations):
    elements = unknowns.shape[2]
    outer_trace = jnp.take(extended, neighbour_code.reshape(-1), axis=2)
    which_turn = orientation.reshape(-1)
    rotated = jnp.einsum('qpx,pr->qrx', outer_trace, rotations[0], precision=HIGHEST)
    for turn_h in range(1, 3):
        turned = jnp.einsum('qpx,pr->qrx', outer_trace, rotations[turn_h], precision=HIGHEST)
        rotated = jnp.where(which_turn == turn_h, turned, rotated)
    normal_flat = jnp.transpose(face_normals, (1, 0, 2)).reshape(3, 4 * elements)
    material_flat = jnp.tile(materials, (1, 4))
    wave_speed = jnp.sqrt((material_flat[0] + 2.0 * material_flat[1]) / material_flat[2])
    wave_speed = wave_speed * jnp.sqrt(lax.optimization_barrier(jnp.sum(normal_flat * normal_flat, axis=0)))
    numeric_flux = 0.5 * elastic(own_table + rotated, normal_flat, material_flat) + 0.5 * wave_speed * (own_table - rotated)
    own_fault = jnp.take(own_table, fault_face, axis=2)
    far_fault = jnp.take(rotated, fault_face, axis=2)
    dip_polar = fault_dip[0]
    dip_azimuth = fault_dip[1]
    unit_normal = (jnp.sin(dip_polar) * jnp.cos(dip_azimuth), jnp.sin(dip_polar) * jnp.sin(dip_azimuth), jnp.cos(dip_polar))
    mean_stress = 0.5 * (own_fault[:6] + far_fault[:6])
    force_vec = traction(mean_stress, unit_normal)
    normal_force = force_vec[0] * unit_normal[0] + force_vec[1] * unit_normal[1] + force_vec[2] * unit_normal[2]
    tangent = jnp.stack([force_vec[axis_c] - normal_force * unit_normal[axis_c] for axis_c in range(3)])
    strength = cohesion + FRICTION * jnp.maximum(-normal_force, 0.0)
    magnitude = jnp.sqrt(lax.optimization_barrier(jnp.sum(tangent * tangent, axis=0)))
    keep_share = strength / jnp.maximum(magnitude, strength)
    excess = (1.0 - keep_share) * tangent
    fault_material = jnp.take(material_flat, fault_face, axis=1)
    numeric_flux = numeric_flux.at[6:9, :, fault_face].add(-excess / fault_material[2])
    lifted = jnp.einsum('qpie,ipb->qbe', numeric_flux.reshape(numeric_flux.shape[0], numeric_flux.shape[1], 4, elements), lifting, precision=HIGHEST)
    updated = jnp.where(live_rows, unknowns + volume_term - lifted, unknowns)
    slip_rate = excess / jnp.sqrt(fault_material[1] * fault_material[2])
    return (updated, slip_rate)

def reference(unknowns, gradients, face_normals, materials, live_count, neighbour_code, orientation, send_face, fault_face, fault_dip, cohesion, stiffness, projection, lifting, rotations):
    devices = N_DOM * N_SUB

    def split_cols(values):
        column_count = values.shape[-1] // devices
        reshaped = values.reshape(values.shape[:-1] + (devices, column_count))
        return jnp.moveaxis(reshaped, -2, 0)

    def join_cols(values):
        reshaped = jnp.moveaxis(values, 0, -2)
        return reshaped.reshape(reshaped.shape[:-2] + (-1,))
    state_dev = split_cols(unknowns)
    grad_dev = split_cols(gradients)
    normal_dev = split_cols(face_normals)
    material_dev = split_cols(materials)
    neighbour_dev = split_cols(neighbour_code)
    orient_dev = split_cols(orientation)
    send_dev = send_face.reshape(devices, 8, -1)
    fault_dev = fault_face.reshape(devices, -1)
    dip_dev = split_cols(fault_dip)
    cohesion_dev = split_cols(cohesion)
    slip_total = jnp.zeros((devices, 3) + cohesion_dev.shape[1:], jnp.float32)
    for update_step in range(STEPS):

        def first_phase(inputs):
            state_one, grad_one, material_one = inputs
            integrated = predict(state_one, grad_one, material_one, stiffness)
            return (volume(integrated, grad_one, material_one, stiffness), face_traces(integrated, projection))
        volume_all, table_all = lax.map(first_phase, (state_dev, grad_dev, material_dev))

        def second_phase(device):
            dom_pos = device // N_SUB
            sub_pos = device % N_SUB
            blocks = [table_all[device]]
            for block_k, offset in enumerate(OFFSETS):
                source_dom = dom_pos - offset
                has_source = (source_dom >= 0) & (source_dom < N_DOM)
                source = jnp.clip(source_dom, 0, N_DOM - 1) * N_SUB + sub_pos
                picked = jnp.take(table_all[source], send_dev[source, block_k], axis=2)
                blocks.append(jnp.where(has_source, picked, 0.0))
            partner = dom_pos * N_SUB + sub_pos + 1 - 2 * (sub_pos % 2)
            blocks.append(jnp.take(table_all[partner], fault_dev[partner], axis=2))
            extended = jnp.concatenate(blocks, axis=2)
            live_rows = jnp.arange(E_CAP, dtype=jnp.int32) < live_count[device]
            return finish(state_dev[device], volume_all[device], table_all[device], extended, neighbour_dev[device], orient_dev[device], normal_dev[device], material_dev[device], fault_dev[device], dip_dev[device], cohesion_dev[device], live_rows, lifting, rotations)
        state_dev, slip_step = lax.map(second_phase, jnp.arange(devices, dtype=jnp.int32))
        slip_total = slip_total + slip_step
    return (join_cols(state_dev), join_cols(slip_total))
```

```python
import functools

import jax
import jax.numpy as jnp
from jax import lax
from jax.experimental import pallas as pl
from jax.experimental.pallas import tpu as pltpu
from jax.sharding import PartitionSpec as P

STEPS = 2
DEGREES = 4
OFFSETS = (1, 2, 3, 4, -1, -2, -3, -4)
FRICTION = 0.6
HIGHEST = lax.Precision.HIGHEST
MESH = pl.DeviceIdType.MESH

F32 = jnp.float32
BF16 = jnp.bfloat16
Q = 9
B = 35
BP = 40
PTS = 15
PP = 16
E = 256
SLOTS = 256
ROWS = Q * PP


def iota(shape, dim):
    return lax.broadcasted_iota(jnp.int32, shape, dim)


def exact_dot(a, b, dims=(((1,), (0,)), ((), ()))):
    return lax.dot_general(a, b, dims, precision=HIGHEST, preferred_element_type=F32)


def fast_dot(a, b):
    return lax.dot_general(a, b, (((1,), (0,)), ((), ())), preferred_element_type=F32)


def halves(x):
    hi = x.astype(BF16).astype(F32)
    return hi, x - hi


def elastic_rows(s, n, m):
    px, py, pz = s[6] * n[0], s[7] * n[1], s[8] * n[2]
    pressure = m[0] * (px + py + pz)
    return (
        pressure + m[1] * px,
        pressure + m[1] * py,
        pressure + m[1] * pz,
        m[2] * (s[6] * n[1] + s[7] * n[0]),
        m[2] * (s[7] * n[2] + s[8] * n[1]),
        m[2] * (s[6] * n[2] + s[8] * n[0]),
        m[3] * (s[0] * n[0] + s[3] * n[1] + s[5] * n[2]),
        m[3] * (s[3] * n[0] + s[1] * n[1] + s[4] * n[2]),
        m[3] * (s[5] * n[0] + s[4] * n[1] + s[2] * n[2]),
    )


def traction(s, n):
    return (
        s[0] * n[0] + s[3] * n[1] + s[5] * n[2],
        s[3] * n[0] + s[1] * n[1] + s[4] * n[2],
        s[5] * n[0] + s[4] * n[1] + s[2] * n[2],
    )


def kernel(
    n_dom,
    un, gr, fn, mat, live, nc, ori, sf, ff, dip, coh, st, pj, lf, ro,
    out, slip,
    state, cur, integ, R, tr, ths, rt, fx, p1, p2, sp, sg, hs,
    lsf, lpred, lvol, lprj, llift, lrot, coef, fcoef, turn, scoef, fric, slipsum,
    sendb, recvb, sendf, recvf,
    send_sem, recv_sem, fsend_sem, frecv_sem,
):
    me = lax.axis_index("dom")
    sub = lax.axis_index("sub")
    partner = sub + 1 - 2 * (sub % 2)

    barrier = pltpu.get_barrier_semaphore()
    for o in OFFSETS:
        dst = me + o

        @pl.when((dst >= 0) & (dst < n_dom))
        def _():
            pl.semaphore_signal(barrier, inc=1, device_id=(dst, sub), device_id_type=MESH)

    pl.semaphore_signal(barrier, inc=1, device_id=(me, partner), device_id_type=MESH)

    for k, o in enumerate(OFFSETS):
        src = me - o

        @pl.when((src < 0) | (src >= n_dom))
        def _():
            for step in range(STEPS):
                recvb[step, k] = jnp.zeros(recvb.shape[2:], F32)

    rep = (iota((B, 128), 0) == iota((B, 128), 1) % BP) & (iota((B, 128), 1) < 3 * BP)
    rep = jnp.where(rep, 1.0, 0.0)
    low_part = iota((128, 128), 1) >= 2 * BP
    TN = (((0,), (0,)), ((), ()))

    def stacked(x, low):
        hi, lo = halves(x)
        return jnp.where(low, lo, hi).astype(BF16)

    lsf[...] = jnp.zeros_like(lsf)
    for d in range(3):
        lsf[BP * d:BP * d + B, :] = exact_dot(st[d], rep, TN)
    lpred[...] = stacked(lsf[...], low_part)
    for d in range(3):
        lsf[BP * d:BP * d + B, :] = exact_dot(st[d], rep)
    lvol[...] = stacked(lsf[...], low_part)
    lsf[...] = jnp.zeros_like(lsf)
    for i in range(4):
        lsf[PP * i:PP * i + PTS, :] = exact_dot(pj[i], rep, TN)
    lprj[...] = stacked(lsf[0:4 * PP, :], low_part[0:4 * PP])
    total = jnp.zeros((B, 12 * PP), F32)
    for i in range(4):
        place = iota((PTS, 12 * PP), 1) % (4 * PP) == iota((PTS, 12 * PP), 0) + PP * i
        total = total + exact_dot(lf[i], jnp.where(place, 1.0, 0.0), TN)
    total = jnp.concatenate([total, jnp.zeros((48 - B, 12 * PP), F32)], axis=0)
    llift[...] = stacked(total, iota((48, 12 * PP), 1) >= 8 * PP)
    place = jnp.where(iota((PTS, 3 * PP), 1) % PP == iota((PTS, 3 * PP), 0), 1.0, 0.0)
    pad = jnp.zeros((PP - PTS, 3 * PP), F32)
    turns = []
    for h in range(3):
        turns += [exact_dot(ro[h], place, TN), pad]
    lrot[...] = stacked(jnp.concatenate(turns, axis=0), iota((3 * PP, 3 * PP), 1) >= 2 * PP)

    def spread(row):
        return jnp.broadcast_to(row, (8, E))

    lam, mu, rho = mat[0:1, :], mat[1:2, :], mat[2:3, :]
    for d in range(3):
        for c in range(3):
            coef[3 * d + c] = spread(gr[d, c:c + 1, :])
    inv_rho = 1.0 / rho
    for j, row in enumerate((-lam, -2.0 * mu, -mu, -inv_rho)):
        coef[9 + j] = spread(row)
    speed = 0.5 * jnp.sqrt((lam + 2.0 * mu) / rho)
    slip_scale = 1.0 / jnp.sqrt(mu * rho)
    param_blocks = []
    for i in range(4):
        nx, ny, nz = fn[i, 0:1, :], fn[i, 1:2, :], fn[i, 2:3, :]
        cw = speed * jnp.sqrt(nx * nx + ny * ny + nz * nz)
        rows = [0.5 * nx, 0.5 * ny, 0.5 * nz, cw]
        for j, row in enumerate(rows):
            fcoef[i, j] = spread(row)
        h = ori[i:i + 1, :]
        masks = [jnp.where(h == t, 1.0, 0.0) for t in range(3)]
        turn[i, 0] = spread(masks[0])
        turn[i, 1] = spread(masks[1])
        rows += [-lam, -2.0 * mu, -mu, -inv_rho, slip_scale, masks[0], masks[1], masks[2]]
        which = iota((PP, E), 0)
        block = jnp.zeros((PP, E), F32)
        for j, row in enumerate(rows):
            block = jnp.where(which == j, jnp.broadcast_to(row, (PP, E)), block)
        param_blocks.append(block)

    place_h = jnp.where(
        ((iota((224, SLOTS), 1) & 31) < 28)
        & (iota((224, SLOTS), 0) == 28 * (iota((224, SLOTS), 1) >> 5) + (iota((224, SLOTS), 1) & 31)),
        1.0, 0.0,
    )
    place_f = jnp.where(
        ((iota((32, SLOTS), 1) & 31) >= 28)
        & (iota((32, SLOTS), 0) == 4 * (iota((32, SLOTS), 1) >> 5) + (iota((32, SLOTS), 1) & 31) - 28),
        1.0, 0.0,
    )
    codes = exact_dot(jnp.broadcast_to(sf[...].astype(F32), (8, 224)), place_h)
    codes = codes + exact_dot(jnp.broadcast_to(ff[...].astype(F32), (8, 32)), place_f)
    codes = (codes[0:1, :] + 0.5).astype(jnp.int32)
    for i in range(4):
        sp[E * i:E * i + E, :] = jnp.where(iota((E, SLOTS), 0) + E * i == codes, 1.0, 0.0).astype(BF16)

    slot_params = jnp.zeros((3 * PP, SLOTS), F32)
    for i in range(4):
        code = nc[i:i + 1, :]
        for j in range(4):
            p1[i, E * j:E * j + E, :] = jnp.where(iota((E, E), 0) + E * j == code, 1.0, 0.0).astype(BF16)
        halo = code - 1024
        block = jnp.zeros_like(halo)
        for m in range(1, 8):
            block = block + jnp.where(halo >= 28 * m, 1, 0)
        fault = code - 1248
        spot = jnp.where(fault >= 0, fault + 28 * (fault >> 2) + 28, jnp.where(halo >= 0, halo + 4 * block, -1))
        hot = jnp.where(iota((SLOTS, E), 0) == spot, 1.0, 0.0).astype(BF16)
        p2[i] = hot
        hi, rest = halves(param_blocks[i])
        mid, lo = halves(rest)
        left = jnp.concatenate([hi, mid, lo], axis=0).astype(BF16)
        slot_params = slot_params + lax.dot_general(
            left, hot, (((1,), (1,)), ((), ())), preferred_element_type=F32
        )
    slot_params = slot_params[0:PP] + slot_params[PP:2 * PP] + slot_params[2 * PP:3 * PP]
    for j in range(12):
        scoef[j] = spread(slot_params[j:j + 1, :])

    on_fault = (iota((PP, SLOTS), 1) & 31) >= 28
    angles = exact_dot(dip[...], place_f)
    polar, azimuth = angles[0:1, :], angles[1:2, :]
    fric[0] = jnp.broadcast_to(jnp.sin(polar) * jnp.cos(azimuth), (PP, SLOTS))
    fric[1] = jnp.broadcast_to(jnp.sin(polar) * jnp.sin(azimuth), (PP, SLOTS))
    fric[2] = jnp.broadcast_to(jnp.cos(polar), (PP, SLOTS))
    held = jnp.concatenate([exact_dot(coh[...], place_f), jnp.zeros((PP - PTS, SLOTS), F32)], axis=0)
    fric[3] = jnp.where(on_fault & (iota((PP, SLOTS), 0) < PTS), held, 1.0)
    slipsum[...] = jnp.zeros_like(slipsum)

    for q in range(Q):
        state[q] = jnp.concatenate([un[q], jnp.zeros((BP - B, E), F32)], axis=0)
    live_lane = iota((1, E), 1) < live[0]

    def split_modes(x):
        hi, lo = halves(x)
        return jnp.concatenate([hi, lo, hi, jnp.zeros((8, E), F32)], axis=0).astype(BF16)

    def sum_elastic(store):
        def body(rb, carry):
            def get(q, d):
                return R[q, pl.ds(pl.multiple_of(BP * d + 8 * rb, 8), 8), :]

            g = [[coef[3 * d + c] for c in range(3)] for d in range(3)]
            m = [coef[9 + j] for j in range(4)]
            grad = {}
            for i in range(3):
                v = [get(6 + i, d) for d in range(3)]
                for c in range(3):
                    grad[i, c] = v[0] * g[0][c] + v[1] * g[1][c] + v[2] * g[2][c]
            pressure = m[0] * (grad[0, 0] + grad[1, 1] + grad[2, 2])
            res = [
                pressure + m[1] * grad[0, 0],
                pressure + m[1] * grad[1, 1],
                pressure + m[1] * grad[2, 2],
                m[2] * (grad[0, 1] + grad[1, 0]),
                m[2] * (grad[1, 2] + grad[2, 1]),
                m[2] * (grad[0, 2] + grad[2, 0]),
            ]
            for kinds in ((0, 3, 5), (3, 1, 4), (5, 4, 2)):
                force = None
                for c, q in enumerate(kinds):
                    for d in range(3):
                        term = get(q, d) * g[d][c]
                        force = term if force is None else force + term
                res.append(m[3] * force)
            store(pl.ds(pl.multiple_of(8 * rb, 8), 8), res)
            return carry

        lax.fori_loop(0, BP // 8, body, 0, unroll=True)

    def send(step, k):
        return pltpu.make_async_remote_copy(
            src_ref=sendb.at[step, k],
            dst_ref=recvb.at[step, k],
            send_sem=send_sem.at[step, k],
            recv_sem=recv_sem.at[step, k],
            device_id=(me + OFFSETS[k], sub),
            device_id_type=MESH,
        )

    def send_fault(step):
        return pltpu.make_async_remote_copy(
            src_ref=sendf.at[step],
            dst_ref=recvf.at[step],
            send_sem=fsend_sem.at[step],
            recv_sem=frecv_sem.at[step],
            device_id=(me, partner),
            device_id_type=MESH,
        )

    def update(step, carry):
        factor = 1.0
        for degree in range(1, DEGREES + 1):
            source = state if degree == 1 else cur
            for q in range(Q):
                R[q] = fast_dot(lpred[...], split_modes(source[q]))
            factor = factor / (degree + 1)
            base = state if degree == 1 else integ

            def store(rows, res, factor=factor, base=base):
                for q in range(Q):
                    cur[q, rows, :] = res[q]
                    integ[q, rows, :] = base[q, rows, :] + factor * res[q]

            sum_elastic(store)

        for q in range(Q):
            t = fast_dot(lprj[...], split_modes(integ[q]))
            tr[q] = t
            hi, lo = halves(t)
            hi = hi.astype(BF16)
            lo = lo.astype(BF16)
            for i in range(4):
                ths[PP * q:PP * q + PP, E * i:E * i + E] = hi[PP * i:PP * i + PP]
                ths[ROWS + PP * q:ROWS + PP * q + PP, E * i:E * i + E] = lo[PP * i:PP * i + PP]

        picked = fast_dot(ths[...], sp[...])
        picked = picked[0:ROWS] + picked[ROWS:2 * ROWS]
        sg[...] = picked
        main = jnp.transpose(picked[0:128])
        rest = picked[128:ROWS]
        for k in range(8):
            sendb[step, k, 0:32, :] = main[32 * k:32 * k + 32]
            sendb[step, k, 32:48, :] = rest[:, 128 * (k // 4):128 * (k // 4) + 128]
            sendf[step, 8 * k:8 * k + 8, :] = main[32 * k + 24:32 * k + 32]
        for t in range(2):
            sendf[step, 64 + 16 * t:80 + 16 * t, :] = rest[:, 128 * t:128 * t + 128]

        @pl.when(step == 0)
        def _():
            pl.semaphore_wait(barrier, 1 + jnp.minimum(me, 4) + jnp.minimum(n_dom - 1 - me, 4))

        for k, o in enumerate(OFFSETS):
            dst = me + o

            @pl.when((dst >= 0) & (dst < n_dom))
            def _():
                send(step, k).start()

        send_fault(step).start()

        def own_face(i, c):
            g = fast_dot(ths[...], p1[i]).astype(BF16)
            m0, m1 = turn[i, 0] > 0.5, turn[i, 1] > 0.5
            for q in range(Q):
                hi = g[PP * q:PP * q + PP]
                lo = g[ROWS + PP * q:ROWS + PP * q + PP]
                r = fast_dot(lrot[...], jnp.concatenate([hi, lo, hi], axis=0))
                for half in range(2):
                    a = 8 * half
                    rt[q, pl.ds(pl.multiple_of(PP * i + a, 8), 8), :] = jnp.where(
                        m0, r[a:a + 8], jnp.where(m1, r[PP + a:PP + a + 8], r[2 * PP + a:2 * PP + a + 8])
                    )
            m = [coef[9 + j] for j in range(4)]
            n = [fcoef[i, j] for j in range(3)]
            cw = fcoef[i, 3]
            for half in range(2):
                rows = pl.ds(pl.multiple_of(PP * i + 8 * half, 8), 8)
                own = [tr[q, rows, :] for q in range(Q)]
                far = [rt[q, rows, :] for q in range(Q)]
                res = elastic_rows([x + y for x, y in zip(own, far)], n, m)
                for q in range(Q):
                    fx[q, rows, :] = res[q] + cw * (own[q] - far[q])
            return c

        lax.fori_loop(0, 4, own_face, 0, unroll=True)

        for q in range(Q):
            R[q] = fast_dot(lvol[...], split_modes(integ[q]))

        def store_volume(rows, res):
            for q in range(Q):
                cur[q, rows, :] = state[q, rows, :] + res[q]

        sum_elastic(store_volume)
        for q in range(Q):
            hi, lo = halves(fx[q])
            lifted = fast_dot(llift[...], jnp.concatenate([hi, lo, hi], axis=0).astype(BF16))
            cur[q] = cur[q] - lifted[0:BP]

        for k, o in enumerate(OFFSETS):
            src = me - o

            @pl.when((src >= 0) & (src < n_dom))
            def _():
                send(step, k).wait_recv()

        send_fault(step).wait_recv()
        blocks = []
        lower = iota((8, 128), 0) >= 4
        for k in range(8):
            blocks.append(recvb[step, k, 0:24, :])
            blocks.append(jnp.where(lower, recvf[step, 8 * k:8 * k + 8, :], recvb[step, k, 24:32, :]))
        main = jnp.transpose(jnp.concatenate(blocks, axis=0))
        lane = iota((PP, 128), 1)
        tails = []
        for t in range(2):
            tail = recvb[step, 4 * t, 32:48, :]
            for j in range(1, 4):
                tail = jnp.where((lane >> 5) == j, recvb[step, 4 * t + j, 32:48, :], tail)
            tails.append(jnp.where((lane & 31) >= 28, recvf[step, 64 + 16 * t:80 + 16 * t, :], tail))
        tail = jnp.concatenate(tails, axis=1)

        far = []
        m0 = jnp.concatenate([scoef[9], scoef[9]], axis=0) > 0.5
        m1 = jnp.concatenate([scoef[10], scoef[10]], axis=0) > 0.5
        for q in range(Q):
            x = main[PP * q:PP * q + PP] if q < 8 else tail
            hi, lo = halves(x)
            r = fast_dot(lrot[...], jnp.concatenate([hi, lo, hi], axis=0).astype(BF16))
            far.append(jnp.where(m0, r[0:PP], jnp.where(m1, r[PP:2 * PP], r[2 * PP:3 * PP])))

        def double(j):
            return jnp.concatenate([scoef[j], scoef[j]], axis=0)

        n = [double(j) for j in range(3)]
        cw = double(3)
        m = [double(4 + j) for j in range(4)]
        flux = elastic_rows(far, n, m)
        flux = [flux[q] - cw * far[q] for q in range(Q)]

        u = (fric[0], fric[1], fric[2])
        mean = [0.5 * (sg[PP * q:PP * q + PP, :] + far[q]) for q in range(6)]
        force = traction(mean, u)
        along = force[0] * u[0] + force[1] * u[1] + force[2] * u[2]
        tangent = [force[c] - along * u[c] for c in range(3)]
        strength = fric[3] + FRICTION * jnp.maximum(-along, 0.0)
        size = jnp.sqrt(tangent[0] * tangent[0] + tangent[1] * tangent[1] + tangent[2] * tangent[2])
        over = jnp.where(on_fault, 1.0 - strength / jnp.maximum(size, strength), 0.0)
        slip_scale = double(8)
        for c in range(3):
            excess = over * tangent[c]
            flux[6 + c] = flux[6 + c] + excess * m[3]
            slipsum[PP * c:PP * c + PP, :] += excess * slip_scale

        parts = [halves(f) for f in flux]
        left = jnp.concatenate([p[0] for p in parts] + [p[1] for p in parts], axis=0).astype(BF16)
        for i in range(4):
            hs[i] = fast_dot(left, p2[i]).astype(BF16)
        for q in range(Q):
            his = [hs[i, PP * q:PP * q + PP, :] for i in range(4)]
            los = [hs[i, ROWS + PP * q:ROWS + PP * q + PP, :] for i in range(4)]
            lifted = fast_dot(llift[...], jnp.concatenate(his + los + his, axis=0))
            state[q] = jnp.where(live_lane, cur[q] - lifted[0:BP], state[q])

        for k, o in enumerate(OFFSETS):
            dst = me + o

            @pl.when((dst >= 0) & (dst < n_dom))
            def _():
                send(step, k).wait_send()

        send_fault(step).wait_send()
        return carry

    lax.fori_loop(0, STEPS, update, 0)

    for q in range(Q):
        out[q] = state[q, 0:B, :]
    back = jnp.where(
        ((iota((SLOTS, 32), 0) & 31) >= 28)
        & (iota((SLOTS, 32), 1) == 4 * (iota((SLOTS, 32), 0) >> 5) + (iota((SLOTS, 32), 0) & 31) - 28),
        1.0, 0.0,
    )
    gone = exact_dot(slipsum[...], back)
    for c in range(3):
        slip[c] = gone[PP * c:PP * c + PTS]


def on_device(n_dom, *args):
    (un, gr, fn, mat, live, nc, ori, sf, ff, dip, coh, st, pj, lf, ro) = args
    vmem = pl.BlockSpec(memory_space=pltpu.VMEM)
    smem = pl.BlockSpec(memory_space=pltpu.SMEM)

    def f32(*shape):
        return pltpu.VMEM(shape, F32)

    def b16(*shape):
        return pltpu.VMEM(shape, BF16)

    return pl.pallas_call(
        functools.partial(kernel, n_dom),
        out_shape=(
            jax.ShapeDtypeStruct((Q, B, E), F32),
            jax.ShapeDtypeStruct((3, PTS, 32), F32),
        ),
        in_specs=[vmem] * 4 + [smem] + [vmem] * 10,
        out_specs=(vmem, vmem),
        scratch_shapes=[
            f32(Q, BP, E),
            f32(Q, BP, E),
            f32(Q, BP, E),
            f32(Q, 128, E),
            f32(Q, 4 * PP, E),
            b16(2 * ROWS, 4 * E),
            f32(Q, 4 * PP, E),
            f32(Q, 4 * PP, E),
            b16(4, 4 * E, E),
            b16(4, SLOTS, E),
            b16(4 * E, SLOTS),
            f32(ROWS, SLOTS),
            b16(4, 2 * ROWS, E),
            f32(128, 128),
            b16(128, 128),
            b16(128, 128),
            b16(4 * PP, 128),
            b16(48, 12 * PP),
            b16(3 * PP, 3 * PP),
            f32(13, 8, E),
            f32(4, 4, 8, E),
            f32(4, 2, 8, E),
            f32(12, 8, SLOTS),
            f32(4, PP, SLOTS),
            f32(3 * PP, SLOTS),
            f32(STEPS, 8, 48, 128),
            f32(STEPS, 8, 48, 128),
            f32(STEPS, 96, 128),
            f32(STEPS, 96, 128),
            pltpu.SemaphoreType.DMA((STEPS, 8)),
            pltpu.SemaphoreType.DMA((STEPS, 8)),
            pltpu.SemaphoreType.DMA((STEPS,)),
            pltpu.SemaphoreType.DMA((STEPS,)),
        ],
        compiler_params=pltpu.CompilerParams(
            collective_id=0, has_side_effects=True, vmem_limit_bytes=40 * 1024 * 1024
        ),
        name="ader_updates",
    )(un, gr, fn, mat, live, nc, ori, sf.reshape(1, -1), ff.reshape(1, -1), dip, coh, st, pj, lf, ro)


def solution(mesh):
    split3 = P(None, None, ("dom", "sub"))
    split2 = P(None, ("dom", "sub"))
    split1 = P(("dom", "sub"))
    placed = (
        split3, split3, split3, split2, split1, split2, split2, split1, split1, split2, split2,
        P(), P(), P(), P(),
    )
    return jax.shard_map(
        functools.partial(on_device, mesh.shape["dom"]),
        mesh=mesh,
        in_specs=placed,
        out_specs=(split3, split3),
        check_vma=False,
    )
```

```python
import functools

import jax
import jax.numpy as jnp
from jax import lax
from jax.experimental import pallas as pl
from jax.experimental.pallas import tpu as pltpu
from jax.sharding import PartitionSpec as P

STEPS = 2
DEGREES = 4
OFFSETS = (1, 2, 3, 4, -1, -2, -3, -4)
FRICTION = 0.6
HIGHEST = lax.Precision.HIGHEST
MESH = pl.DeviceIdType.MESH

F32 = jnp.float32
BF16 = jnp.bfloat16
Q = 9
B = 35
BP = 40
PTS = 15
PP = 16
E = 256
SLOTS = 256
LANES = 128
FAULTS = 32
ROWS = Q * PP


def iota(shape, dim):
    return lax.broadcasted_iota(jnp.int32, shape, dim)


def exact_dot(a, b, dims=(((1,), (0,)), ((), ()))):
    return lax.dot_general(a, b, dims, precision=HIGHEST, preferred_element_type=F32)


def fast_dot(a, b):
    return lax.dot_general(a, b, (((1,), (0,)), ((), ())), preferred_element_type=F32)


def halves(x):
    hi = x.astype(BF16).astype(F32)
    return hi, x - hi


def elastic_rows(s, n, m):
    px, py, pz = s[6] * n[0], s[7] * n[1], s[8] * n[2]
    pressure = m[0] * (px + py + pz)
    return (
        pressure + m[1] * px,
        pressure + m[1] * py,
        pressure + m[1] * pz,
        m[2] * (s[6] * n[1] + s[7] * n[0]),
        m[2] * (s[7] * n[2] + s[8] * n[1]),
        m[2] * (s[6] * n[2] + s[8] * n[0]),
        m[3] * (s[0] * n[0] + s[3] * n[1] + s[5] * n[2]),
        m[3] * (s[3] * n[0] + s[1] * n[1] + s[4] * n[2]),
        m[3] * (s[5] * n[0] + s[4] * n[1] + s[2] * n[2]),
    )


def traction(s, n):
    return (
        s[0] * n[0] + s[3] * n[1] + s[5] * n[2],
        s[3] * n[0] + s[1] * n[1] + s[4] * n[2],
        s[5] * n[0] + s[4] * n[1] + s[2] * n[2],
    )


def kernel(
    n_dom,
    un_hbm, gr_hbm, fn_hbm, mat_hbm, nc_hbm, ori_hbm, sf_hbm, ff_hbm, dip_hbm, coh_hbm,
    st_hbm, pj_hbm, lf_hbm, ro_hbm,
    out, slip,
    un, gr, fn, mat, nc, ori, sf, ff, dip, coh, st, pj, lf, ro,
    state, cur, integ, R, tr, ths, rt, fx, p1, p2, sp, spf, hs,
    lsf, lpred, lvol, lprj, llift, lrot, coef, fcoef, turn, scoef, fcode, fdip, fric, slipsum,
    sendb, recvb, sendf, recvf,
    in_sem, send_sem, recv_sem, fsend_sem, frecv_sem,
):
    me = lax.axis_index("dom")
    sub = lax.axis_index("sub")
    partner = sub + 1 - 2 * (sub % 2)

    sources = (st_hbm, un_hbm, gr_hbm, mat_hbm, sf_hbm, pj_hbm, ff_hbm, nc_hbm, fn_hbm, ori_hbm,
               dip_hbm, coh_hbm, lf_hbm, ro_hbm)
    targets = (st, un, gr, mat, sf, pj, ff, nc, fn, ori, dip, coh, lf, ro)
    loads = [pltpu.make_async_copy(a, b, in_sem.at[j]) for j, (a, b) in enumerate(zip(sources, targets))]
    for load in loads:
        load.start()

    barrier = pltpu.get_barrier_semaphore()
    for o in OFFSETS:
        dst = me + o

        @pl.when((dst >= 0) & (dst < n_dom))
        def _():
            pl.semaphore_signal(barrier, inc=1, device_id=(dst, sub), device_id_type=MESH)

    pl.semaphore_signal(barrier, inc=1, device_id=(me, partner), device_id_type=MESH)

    for k, o in enumerate(OFFSETS):
        src = me - o

        @pl.when((src < 0) | (src >= n_dom))
        def _():
            for step in range(STEPS):
                recvb[step, 32 * k:32 * k + 32, :] = jnp.zeros((32, 128), F32)

    rep = (iota((B, 128), 0) == iota((B, 128), 1) % BP) & (iota((B, 128), 1) < 3 * BP)
    rep = jnp.where(rep, 1.0, 0.0)
    low_part = iota((128, 128), 1) >= 2 * BP
    TN = (((0,), (0,)), ((), ()))

    def stacked(x, low):
        hi, lo = halves(x)
        return jnp.where(low, lo, hi).astype(BF16)

    def spread(row):
        return jnp.broadcast_to(row, (8, E))

    place_h = jnp.where(
        ((iota((224, SLOTS), 1) & 31) < 28)
        & (iota((224, SLOTS), 0) == 28 * (iota((224, SLOTS), 1) >> 5) + (iota((224, SLOTS), 1) & 31)),
        1.0, 0.0,
    )
    unused = (iota((1, SLOTS), 1) & 31) >= 28
    lsf[...] = jnp.zeros_like(lsf)
    slipsum[...] = jnp.zeros_like(slipsum)

    loads[0].wait()
    for d in range(3):
        lsf[BP * d:BP * d + B, :] = exact_dot(st[d], rep, TN)
    lpred[...] = stacked(lsf[...], low_part)

    loads[1].wait()
    for q in range(Q):
        state[q] = jnp.concatenate([un[q], jnp.zeros((BP - B, E), F32)], axis=0)
    loads[2].wait()
    for d in range(3):
        for c in range(3):
            coef[3 * d + c] = spread(gr[d, c:c + 1, :])
    loads[3].wait()
    lam, mu, rho = mat[0:1, :], mat[1:2, :], mat[2:3, :]
    for j, row in enumerate((-lam, -2.0 * mu, -mu, -1.0 / rho)):
        coef[9 + j] = spread(row)

    loads[4].wait()
    codes = exact_dot(jnp.broadcast_to(sf[...].astype(F32), (8, 224)), place_h)
    codes = jnp.where(unused, -1, (codes[0:1, :] + 0.5).astype(jnp.int32))
    for i in range(4):
        sp[E * i:E * i + E, :] = jnp.where(iota((E, SLOTS), 0) + E * i == codes, 1.0, 0.0).astype(BF16)
    loads[5].wait()
    lsf[...] = jnp.zeros_like(lsf)
    for i in range(4):
        lsf[PP * i:PP * i + PTS, :] = exact_dot(pj[:, i, :], rep)
    lprj[...] = stacked(lsf[0:4 * PP, :], low_part[0:4 * PP])

    def setup_fault():
        loads[6].wait()
        fcode[...] = jnp.full(fcode.shape, -1, jnp.int32)
        fcode[0:1, 0:FAULTS] = ff[...]
        for i in range(4):
            hot = iota((E, LANES), 0) + E * i == fcode[0:1, :]
            spf[E * i:E * i + E, :] = jnp.where(hot, 1.0, 0.0).astype(BF16)

    def setup_rest():
        for load in loads[7:]:
            load.wait()
        for d in range(3):
            lsf[BP * d:BP * d + B, :] = exact_dot(st[d], rep)
        lvol[...] = stacked(lsf[...], low_part)
        total = jnp.zeros((B, 12 * PP), F32)
        for i in range(4):
            place = iota((PTS, 12 * PP), 1) % (4 * PP) == iota((PTS, 12 * PP), 0) + PP * i
            total = total + exact_dot(lf[:, i, :], jnp.where(place, 1.0, 0.0), TN)
        total = jnp.concatenate([total, jnp.zeros((48 - B, 12 * PP), F32)], axis=0)
        llift[...] = stacked(total, iota((48, 12 * PP), 1) >= 8 * PP)
        place = jnp.where(iota((PTS, 3 * PP), 1) % PP == iota((PTS, 3 * PP), 0), 1.0, 0.0)
        pad = jnp.zeros((PP - PTS, 3 * PP), F32)
        turns = []
        for h in range(3):
            turns += [exact_dot(ro[h], place, TN), pad]
        lrot[...] = stacked(jnp.concatenate(turns, axis=0), iota((3 * PP, 3 * PP), 1) >= 2 * PP)

        lam, mu, rho = mat[0:1, :], mat[1:2, :], mat[2:3, :]
        speed = 0.5 * jnp.sqrt((lam + 2.0 * mu) / rho)
        slip_scale = 1.0 / jnp.sqrt(mu * rho)
        slot_params = jnp.zeros((3 * PP, SLOTS + LANES), F32)
        for i in range(4):
            nx, ny, nz = fn[0, i:i + 1, :], fn[1, i:i + 1, :], fn[2, i:i + 1, :]
            cw = speed * jnp.sqrt(nx * nx + ny * ny + nz * nz)
            rows = [0.5 * nx, 0.5 * ny, 0.5 * nz, cw]
            for j, row in enumerate(rows):
                fcoef[i, j] = spread(row)
            h = ori[i:i + 1, :]
            m0 = jnp.where(h == 0, 1.0, 0.0)
            m1 = jnp.where(h == 1, 1.0, 0.0)
            turn[i, 0] = spread(m0)
            turn[i, 1] = spread(m1)
            rows += [-lam, -2.0 * mu, -mu, -1.0 / rho, slip_scale, m0, m1]
            which = iota((PP, E), 0)
            block = jnp.zeros((PP, E), F32)
            for j, row in enumerate(rows):
                block = jnp.where(which == j, jnp.broadcast_to(row, (PP, E)), block)

            code = nc[i:i + 1, :]
            for j in range(4):
                p1[i, E * j:E * j + E, :] = jnp.where(iota((E, E), 0) + E * j == code, 1.0, 0.0).astype(BF16)
            halo = code - 1024
            number = jnp.zeros_like(halo)
            for m in range(1, 8):
                number = number + jnp.where(halo >= 28 * m, 1, 0)
            fault = code - 1248
            spot = jnp.where(fault >= 0, fault + SLOTS, jnp.where(halo >= 0, halo + 4 * number, -1))
            hot = jnp.where(iota((SLOTS + LANES, E), 0) == spot, 1.0, 0.0).astype(BF16)
            p2[i] = hot
            hi, rest = halves(block)
            mid, lo = halves(rest)
            left = jnp.concatenate([hi, mid, lo], axis=0).astype(BF16)
            slot_params = slot_params + lax.dot_general(
                left, hot, (((1,), (1,)), ((), ())), preferred_element_type=F32
            )
        slot_params = slot_params[0:PP] + slot_params[PP:2 * PP] + slot_params[2 * PP:3 * PP]
        for j in range(11):
            scoef[j] = jnp.broadcast_to(slot_params[j:j + 1, :], (8, SLOTS + LANES))

        fdip[...] = jnp.zeros_like(fdip)
        fdip[0:2, 0:FAULTS] = dip[...]
        polar, azimuth = fdip[0:1, :], fdip[1:2, :]
        fric[0] = jnp.broadcast_to(jnp.sin(polar) * jnp.cos(azimuth), (PP, LANES))
        fric[1] = jnp.broadcast_to(jnp.sin(polar) * jnp.sin(azimuth), (PP, LANES))
        fric[2] = jnp.broadcast_to(jnp.cos(polar), (PP, LANES))
        fric[3] = jnp.ones((PP, LANES), F32)
        fric[3, 0:PTS, 0:FAULTS] = coh[...]

    def split_modes(x):
        hi, lo = halves(x)
        return jnp.concatenate([hi, lo, hi, jnp.zeros((8, E), F32)], axis=0).astype(BF16)

    def sum_elastic(store):
        def body(rb, carry):
            def get(q, d):
                return R[q, pl.ds(pl.multiple_of(BP * d + 8 * rb, 8), 8), :]

            g = [[coef[3 * d + c] for c in range(3)] for d in range(3)]
            m = [coef[9 + j] for j in range(4)]
            grad = {}
            for i in range(3):
                v = [get(6 + i, d) for d in range(3)]
                for c in range(3):
                    grad[i, c] = v[0] * g[0][c] + v[1] * g[1][c] + v[2] * g[2][c]
            pressure = m[0] * (grad[0, 0] + grad[1, 1] + grad[2, 2])
            res = [
                pressure + m[1] * grad[0, 0],
                pressure + m[1] * grad[1, 1],
                pressure + m[1] * grad[2, 2],
                m[2] * (grad[0, 1] + grad[1, 0]),
                m[2] * (grad[1, 2] + grad[2, 1]),
                m[2] * (grad[0, 2] + grad[2, 0]),
            ]
            for kinds in ((0, 3, 5), (3, 1, 4), (5, 4, 2)):
                force = None
                for c, q in enumerate(kinds):
                    for d in range(3):
                        term = get(q, d) * g[d][c]
                        force = term if force is None else force + term
                res.append(m[3] * force)
            store(pl.ds(pl.multiple_of(8 * rb, 8), 8), res)
            return carry

        lax.fori_loop(0, BP // 8, body, 0, unroll=True)

    def send(step, k):
        return pltpu.make_async_remote_copy(
            src_ref=sendb.at[step, pl.ds(32 * k, 32)],
            dst_ref=recvb.at[step, pl.ds(32 * k, 32)],
            send_sem=send_sem.at[step, k],
            recv_sem=recv_sem.at[step, k],
            device_id=(me + OFFSETS[k], sub),
            device_id_type=MESH,
        )

    def send_fault(step):
        return pltpu.make_async_remote_copy(
            src_ref=sendf.at[step],
            dst_ref=recvf.at[step],
            send_sem=fsend_sem.at[step],
            recv_sem=frecv_sem.at[step],
            device_id=(me, partner),
            device_id_type=MESH,
        )

    def shifted(x, by):
        return jnp.concatenate(
            [pltpu.roll(x[:, LANES * t:LANES * t + LANES], by % LANES, 1) for t in range(SLOTS // LANES)], axis=1
        )

    in_block = iota((8, SLOTS), 1) & 31
    last_row = iota((8, SLOTS), 0) == 7

    def turned(x, first, second):
        r = fast_dot(lrot[...], jnp.concatenate([x[0], x[1], x[0]], axis=0))
        return jnp.where(first, r[0:PP], jnp.where(second, r[PP:2 * PP], r[2 * PP:3 * PP]))

    def both(x):
        hi, lo = halves(x)
        return hi.astype(BF16), lo.astype(BF16)

    def slot_coefs(lanes):
        def double(j):
            return jnp.concatenate([scoef[j, :, lanes], scoef[j, :, lanes]], axis=0)

        return [double(j) for j in range(11)]

    def outer_flux(far, c):
        flux = elastic_rows(far, c[0:3], c[4:8])
        return [flux[q] - c[3] * far[q] for q in range(Q)]

    def stacked_rows(flux):
        parts = [halves(f) for f in flux]
        return jnp.concatenate([p[0] for p in parts] + [p[1] for p in parts], axis=0).astype(BF16)

    def update(step, carry):
        factor = 1.0
        for degree in range(1, DEGREES + 1):
            source = state if degree == 1 else cur
            for q in range(Q):
                R[q] = fast_dot(lpred[...], split_modes(source[q]))
            factor = factor / (degree + 1)
            base = state if degree == 1 else integ

            def store(rows, res, factor=factor, base=base):
                for q in range(Q):
                    cur[q, rows, :] = res[q]
                    integ[q, rows, :] = base[q, rows, :] + factor * res[q]

            sum_elastic(store)

        for q in range(Q):
            t = fast_dot(lprj[...], split_modes(integ[q]))
            tr[q] = t
            hi, lo = both(t)
            for i in range(4):
                ths[PP * q:PP * q + PP, E * i:E * i + E] = hi[PP * i:PP * i + PP]
                ths[ROWS + PP * q:ROWS + PP * q + PP, E * i:E * i + E] = lo[PP * i:PP * i + PP]

        picked = fast_dot(ths[...], sp[...])
        picked = picked[0:ROWS] + picked[ROWS:2 * ROWS]
        tail = picked[128 + 8:ROWS]
        tiles = []
        for t in range(16):
            x = picked[8 * t:8 * t + 8]
            if t % 2 == 1:
                x = jnp.where(last_row, jnp.broadcast_to(picked[128 + t // 2:129 + t // 2], (8, SLOTS)), x)
            if t < 7:
                x = jnp.where(in_block >= 28, shifted(tail, 28 - 4 * t), x)
            tiles.append(x)
        sendb[step] = jnp.transpose(jnp.concatenate(tiles, axis=0))

        @pl.when(step == 0)
        def _():
            pl.semaphore_wait(barrier, 1 + jnp.minimum(me, 4) + jnp.minimum(n_dom - 1 - me, 4))

        for k in (3, 7, 2, 6, 1, 5, 0, 4):
            dst = me + OFFSETS[k]

            @pl.when((dst >= 0) & (dst < n_dom))
            def _():
                send(step, k).start()

        @pl.when(step == 0)
        def _():
            setup_fault()

        picked = fast_dot(ths[...], spf[...])
        sendf[step] = picked[0:ROWS] + picked[ROWS:2 * ROWS]
        send_fault(step).start()

        @pl.when(step == 0)
        def _():
            setup_rest()

        def own_face(i, c):
            g = fast_dot(ths[...], p1[i]).astype(BF16)
            m0, m1 = turn[i, 0] > 0.5, turn[i, 1] > 0.5
            for q in range(Q):
                hi = g[PP * q:PP * q + PP]
                lo = g[ROWS + PP * q:ROWS + PP * q + PP]
                r = fast_dot(lrot[...], jnp.concatenate([hi, lo, hi], axis=0))
                for half in range(2):
                    a = 8 * half
                    rt[q, pl.ds(pl.multiple_of(PP * i + a, 8), 8), :] = jnp.where(
                        m0, r[a:a + 8], jnp.where(m1, r[PP + a:PP + a + 8], r[2 * PP + a:2 * PP + a + 8])
                    )
            m = [coef[9 + j] for j in range(4)]
            n = [fcoef[i, j] for j in range(3)]
            cw = fcoef[i, 3]
            for half in range(2):
                rows = pl.ds(pl.multiple_of(PP * i + 8 * half, 8), 8)
                own = [tr[q, rows, :] for q in range(Q)]
                far = [rt[q, rows, :] for q in range(Q)]
                res = elastic_rows([x + y for x, y in zip(own, far)], n, m)
                for q in range(Q):
                    fx[q, rows, :] = res[q] + cw * (own[q] - far[q])
            return c

        lax.fori_loop(0, 4, own_face, 0, unroll=True)

        for q in range(Q):
            R[q] = fast_dot(lvol[...], split_modes(integ[q]))

        def store_volume(rows, res):
            for q in range(Q):
                cur[q, rows, :] = state[q, rows, :] + res[q]

        sum_elastic(store_volume)

        send_fault(step).wait_recv()
        c = slot_coefs(slice(SLOTS, SLOTS + LANES))
        first, second = c[9] > 0.5, c[10] > 0.5
        far = [turned(both(recvf[step, PP * q:PP * q + PP, :]), first, second) for q in range(Q)]
        flux = outer_flux(far, c)
        u = (fric[0], fric[1], fric[2])
        mean = [0.5 * (sendf[step, PP * q:PP * q + PP, :] + far[q]) for q in range(6)]
        force = traction(mean, u)
        along = force[0] * u[0] + force[1] * u[1] + force[2] * u[2]
        tangent = [force[a] - along * u[a] for a in range(3)]
        strength = fric[3] + FRICTION * jnp.maximum(-along, 0.0)
        size = jnp.sqrt(tangent[0] * tangent[0] + tangent[1] * tangent[1] + tangent[2] * tangent[2])
        over = 1.0 - strength / jnp.maximum(size, strength)
        for a in range(3):
            excess = over * tangent[a]
            flux[6 + a] = flux[6 + a] + excess * c[7]
            slipsum[PP * a:PP * a + PP, :] += excess * c[8]
        left = stacked_rows(flux)
        for i in range(4):
            r = fast_dot(left, p2[i, SLOTS:SLOTS + LANES, :])
            for q in range(Q):
                fx[q, PP * i:PP * i + PP, :] += r[PP * q:PP * q + PP] + r[ROWS + PP * q:ROWS + PP * q + PP]

        for q in range(Q):
            hi, lo = both(fx[q])
            lifted = fast_dot(llift[...], jnp.concatenate([hi, lo, hi], axis=0))
            cur[q] = cur[q] - lifted[0:BP]

        for k, o in enumerate(OFFSETS):
            src = me - o

            @pl.when((src >= 0) & (src < n_dom))
            def _():
                send(step, k).wait_recv()

        main = jnp.transpose(recvb[step])
        tail = jnp.zeros((8, SLOTS), F32)
        for t in range(7):
            tail = jnp.where((in_block >> 2) == t, shifted(main[8 * t:8 * t + 8], 4 * t - 28), tail)
        last = jnp.concatenate([main[PP * q + PTS:PP * q + PP] for q in range(8)] + [tail], axis=0)
        c = slot_coefs(slice(0, SLOTS))
        first, second = c[9] > 0.5, c[10] > 0.5
        far = [
            turned(both(main[PP * q:PP * q + PP] if q < 8 else last), first, second) for q in range(Q)
        ]
        left = stacked_rows(outer_flux(far, c))
        for i in range(4):
            hs[i] = fast_dot(left, p2[i, 0:SLOTS, :]).astype(BF16)
        for q in range(Q):
            his = [hs[i, PP * q:PP * q + PP, :] for i in range(4)]
            los = [hs[i, ROWS + PP * q:ROWS + PP * q + PP, :] for i in range(4)]
            lifted = fast_dot(llift[...], jnp.concatenate(his + los + his, axis=0))
            state[q] = cur[q] - lifted[0:BP]
        return carry

    lax.fori_loop(0, STEPS, update, 0)

    for q in range(Q):
        out[q] = state[q, 0:B, :]
    for a in range(3):
        slip[a] = slipsum[PP * a:PP * a + PTS, 0:FAULTS]

    for step in range(STEPS):
        for k, o in enumerate(OFFSETS):
            dst = me + o

            @pl.when((dst >= 0) & (dst < n_dom))
            def _():
                send(step, k).wait_send()

        send_fault(step).wait_send()


def on_device(n_dom, *args):
    (un, gr, fn, mat, live, nc, ori, sf, ff, dip, coh, st, pj, lf, ro) = args
    fn = jnp.transpose(fn, (1, 0, 2))
    pj = jnp.transpose(pj, (2, 0, 1))
    lf = jnp.transpose(lf, (1, 0, 2))
    args = (un, gr, fn, mat, nc, ori, sf.reshape(1, -1), ff.reshape(1, -1), dip, coh, st, pj, lf, ro)
    vmem = pl.BlockSpec(memory_space=pltpu.VMEM)
    args = [pltpu.with_memory_space_constraint(a, pltpu.HBM) for a in args]

    def f32(*shape):
        return pltpu.VMEM(shape, F32)

    def b16(*shape):
        return pltpu.VMEM(shape, BF16)

    updated, slip = pl.pallas_call(
        functools.partial(kernel, n_dom),
        out_shape=(
            jax.ShapeDtypeStruct((Q, B, E), F32),
            jax.ShapeDtypeStruct((3, PTS, FAULTS), F32),
        ),
        in_specs=[pl.BlockSpec(memory_space=pltpu.HBM)] * len(args),
        out_specs=(vmem, vmem),
        scratch_shapes=[pltpu.VMEM(a.shape, a.dtype) for a in args] + [
            f32(Q, BP, E),
            f32(Q, BP, E),
            f32(Q, BP, E),
            f32(Q, 128, E),
            f32(Q, 4 * PP, E),
            b16(2 * ROWS, 4 * E),
            f32(Q, 4 * PP, E),
            f32(Q, 4 * PP, E),
            b16(4, 4 * E, E),
            b16(4, SLOTS + LANES, E),
            b16(4 * E, SLOTS),
            b16(4 * E, LANES),
            b16(4, 2 * ROWS, E),
            f32(128, 128),
            b16(128, 128),
            b16(128, 128),
            b16(4 * PP, 128),
            b16(48, 12 * PP),
            b16(3 * PP, 3 * PP),
            f32(13, 8, E),
            f32(4, 4, 8, E),
            f32(4, 2, 8, E),
            f32(11, 8, SLOTS + LANES),
            pltpu.VMEM((8, LANES), jnp.int32),
            f32(8, LANES),
            f32(4, PP, LANES),
            f32(3 * PP, LANES),
            f32(STEPS, SLOTS, LANES),
            f32(STEPS, SLOTS, LANES),
            f32(STEPS, ROWS, LANES),
            f32(STEPS, ROWS, LANES),
            pltpu.SemaphoreType.DMA((len(args),)),
            pltpu.SemaphoreType.DMA((STEPS, 8)),
            pltpu.SemaphoreType.DMA((STEPS, 8)),
            pltpu.SemaphoreType.DMA((STEPS,)),
            pltpu.SemaphoreType.DMA((STEPS,)),
        ],
        compiler_params=pltpu.CompilerParams(
            collective_id=0, has_side_effects=True, vmem_limit_bytes=40 * 1024 * 1024
        ),
        name="ader_updates",
    )(*args)
    return jnp.where(iota((1, 1, E), 2) < live[0], updated, un), slip


def solution(mesh):
    split3 = P(None, None, ("dom", "sub"))
    split2 = P(None, ("dom", "sub"))
    split1 = P(("dom", "sub"))
    placed = (
        split3, split3, split3, split2, split1, split2, split2, split1, split1, split2, split2,
        P(), P(), P(), P(),
    )
    return jax.shard_map(
        functools.partial(on_device, mesh.shape["dom"]),
        mesh=mesh,
        in_specs=placed,
        out_specs=(split3, split3),
        check_vma=False,
    )
```

```python
import functools

import jax
import jax.numpy as jnp
from jax import lax
from jax.experimental import pallas as pl
from jax.experimental.pallas import tpu as pltpu
from jax.sharding import PartitionSpec as P

STEPS = 2
DEGREES = 4
OFFSETS = (1, 2, 3, 4, -1, -2, -3, -4)
FRICTION = 0.6
HIGHEST = lax.Precision.HIGHEST
MESH = pl.DeviceIdType.MESH

F32 = jnp.float32
BF16 = jnp.bfloat16
Q = 9
B = 35
BP = 40
PTS = 15
PP = 16
E = 256
SLOTS = 256
LANES = 128
FAULTS = 32
ROWS = Q * PP


def iota(shape, dim):
    return lax.broadcasted_iota(jnp.int32, shape, dim)


def exact_dot(a, b, dims=(((1,), (0,)), ((), ()))):
    return lax.dot_general(a, b, dims, precision=HIGHEST, preferred_element_type=F32)


def fast_dot(a, b, dims=(((1,), (0,)), ((), ()))):
    return lax.dot_general(a, b, dims, preferred_element_type=F32)


def halves(x):
    hi = x.astype(BF16).astype(F32)
    return hi, x - hi


def elastic_rows(s, n, m):
    px, py, pz = s[6] * n[0], s[7] * n[1], s[8] * n[2]
    pressure = m[0] * (px + py + pz)
    return (
        pressure + m[1] * px,
        pressure + m[1] * py,
        pressure + m[1] * pz,
        m[2] * (s[6] * n[1] + s[7] * n[0]),
        m[2] * (s[7] * n[2] + s[8] * n[1]),
        m[2] * (s[6] * n[2] + s[8] * n[0]),
        m[3] * (s[0] * n[0] + s[3] * n[1] + s[5] * n[2]),
        m[3] * (s[3] * n[0] + s[1] * n[1] + s[4] * n[2]),
        m[3] * (s[5] * n[0] + s[4] * n[1] + s[2] * n[2]),
    )


def traction(s, n):
    return (
        s[0] * n[0] + s[3] * n[1] + s[5] * n[2],
        s[3] * n[0] + s[1] * n[1] + s[4] * n[2],
        s[5] * n[0] + s[4] * n[1] + s[2] * n[2],
    )


def kernel(
    n_dom,
    un_hbm, gr_hbm, fn_hbm, mat_hbm, nc_hbm, ori_hbm, sf_hbm, ff_hbm, dip_hbm, coh_hbm,
    st_hbm, pj_hbm, lf_hbm, ro_hbm,
    out, slip,
    un, gr, fn, mat, nc, ori, sf, ff, dip, coh, st, pj, lf, ro,
    state, cur, integ, R, tr, ths, rt, fx, p1, p2, sp, spf, hs,
    lsf, lsp, lpred, lvol, lprj, llift, lrot, coef, fcoef, turn, scoef, fcode, fdip, fric, slipsum,
    sendb, recvb, sendf, recvf,
    in_sem, send_sem, recv_sem, fsend_sem, frecv_sem,
):
    me = lax.axis_index("dom")
    sub = lax.axis_index("sub")
    partner = sub + 1 - 2 * (sub % 2)

    sources = (st_hbm, un_hbm, gr_hbm, mat_hbm, sf_hbm, pj_hbm, ff_hbm, nc_hbm, fn_hbm, ori_hbm,
               dip_hbm, coh_hbm, lf_hbm, ro_hbm)
    targets = (st, un, gr, mat, sf, pj, ff, nc, fn, ori, dip, coh, lf, ro)
    loads = [pltpu.make_async_copy(a, b, in_sem.at[j]) for j, (a, b) in enumerate(zip(sources, targets))]
    for load in loads:
        load.start()

    barrier = pltpu.get_barrier_semaphore()
    for o in OFFSETS:
        dst = me + o

        @pl.when((dst >= 0) & (dst < n_dom))
        def _():
            pl.semaphore_signal(barrier, inc=1, device_id=(dst, sub), device_id_type=MESH)

    pl.semaphore_signal(barrier, inc=1, device_id=(me, partner), device_id_type=MESH)

    for k, o in enumerate(OFFSETS):
        src = me - o

        @pl.when((src < 0) | (src >= n_dom))
        def _():
            for step in range(STEPS):
                recvb[step, 32 * k:32 * k + 32, :] = jnp.zeros((32, 128), F32)

    rep = (iota((B, 128), 0) == iota((B, 128), 1) % BP) & (iota((B, 128), 1) < 3 * BP)
    low_part = iota((B, 128), 1) >= 2 * BP
    rep_hi = jnp.where(rep & ~low_part, 1.0, 0.0).astype(BF16)
    rep_lo = jnp.where(rep & low_part, 1.0, 0.0).astype(BF16)
    row, col = iota((2 * BP, 128), 0), iota((2 * BP, 128), 1)
    rep2 = (row % BP == col % BP) & (row % BP < B) & (col < 3 * BP) & ((row >= BP) == (col >= 2 * BP))
    rep2 = jnp.where(rep2, 1.0, 0.0).astype(BF16)
    TN = (((0,), (0,)), ((), ()))

    def stacked(x, low):
        hi, lo = halves(x)
        return jnp.where(low, lo, hi).astype(BF16)

    def both(x):
        hi, lo = halves(x)
        return hi.astype(BF16), lo.astype(BF16)

    def stack_low(x):
        hi, lo = halves(jnp.concatenate([x, jnp.zeros((BP - B, x.shape[1]), F32)], axis=0))
        return jnp.concatenate([hi, lo], axis=0).astype(BF16)

    def spread(row):
        return jnp.broadcast_to(row, (8, E))

    place_h = jnp.where(
        ((iota((224, SLOTS), 1) & 31) < 28)
        & (iota((224, SLOTS), 0) == 28 * (iota((224, SLOTS), 1) >> 5) + (iota((224, SLOTS), 1) & 31)),
        1.0, 0.0,
    )
    unused = (iota((1, SLOTS), 1) & 31) >= 28
    lsf[...] = jnp.zeros_like(lsf)
    slipsum[...] = jnp.zeros_like(slipsum)

    for load in loads[0:6]:
        load.wait()
    for d in range(3):
        lsf[BP * d:BP * d + B, :] = fast_dot(stack_low(st[d]), rep2, TN)
    lpred[...] = lsf[...].astype(BF16)

    for q in range(Q):
        state[q] = jnp.concatenate([un[q], jnp.zeros((BP - B, E), F32)], axis=0)
    for d in range(3):
        for c in range(3):
            coef[3 * d + c] = spread(gr[d, c:c + 1, :])
    lam, mu, rho = mat[0:1, :], mat[1:2, :], mat[2:3, :]
    for j, row in enumerate((-lam, -2.0 * mu, -mu, -1.0 / rho)):
        coef[9 + j] = spread(row)

    raw = jnp.broadcast_to(sf[...], (8, 224))
    raw = jnp.concatenate([raw >> 8, raw & 255], axis=0).astype(F32).astype(BF16)
    placed = fast_dot(raw, place_h.astype(BF16))
    codes = (placed[0:1, :] * 256.0 + placed[8:9, :] + 0.5).astype(jnp.int32)
    codes = jnp.where(unused, -1, codes)
    for i in range(4):
        sp[E * i:E * i + E, :] = jnp.where(iota((E, SLOTS), 0) + E * i == codes, 1.0, 0.0).astype(BF16)
    lsp[...] = jnp.zeros_like(lsp)
    for i in range(4):
        hi, lo = both(pj[:, i, :])
        lsp[PP * i:PP * i + PTS, :] = fast_dot(hi, rep_hi) + fast_dot(lo, rep_lo)
    lprj[...] = lsp[...].astype(BF16)

    def setup_fault():
        loads[6].wait()
        fcode[...] = jnp.full(fcode.shape, -1, jnp.int32)
        fcode[0:1, 0:FAULTS] = ff[...]
        for i in range(4):
            hot = iota((E, LANES), 0) + E * i == fcode[0:1, :]
            spf[E * i:E * i + E, :] = jnp.where(hot, 1.0, 0.0).astype(BF16)

    def setup_rest():
        for load in loads[7:]:
            load.wait()
        for d in range(3):
            hi, lo = both(st[d])
            lsf[BP * d:BP * d + B, :] = fast_dot(hi, rep_hi) + fast_dot(lo, rep_lo)
        lvol[...] = lsf[...].astype(BF16)
        total = jnp.zeros((B, 12 * PP), F32)
        for i in range(4):
            place = iota((PTS, 12 * PP), 1) % (4 * PP) == iota((PTS, 12 * PP), 0) + PP * i
            total = total + exact_dot(lf[:, i, :], jnp.where(place, 1.0, 0.0), TN)
        total = jnp.concatenate([total, jnp.zeros((48 - B, 12 * PP), F32)], axis=0)
        llift[...] = stacked(total, iota((48, 12 * PP), 1) >= 8 * PP)
        place = jnp.where(iota((PTS, 3 * PP), 1) % PP == iota((PTS, 3 * PP), 0), 1.0, 0.0)
        pad = jnp.zeros((PP - PTS, 3 * PP), F32)
        turns = []
        for h in range(3):
            turns += [exact_dot(ro[h], place, TN), pad]
        lrot[...] = stacked(jnp.concatenate(turns, axis=0), iota((3 * PP, 3 * PP), 1) >= 2 * PP)

        lam, mu, rho = mat[0:1, :], mat[1:2, :], mat[2:3, :]
        speed = 0.5 * jnp.sqrt((lam + 2.0 * mu) / rho)
        slip_scale = 1.0 / jnp.sqrt(mu * rho)
        slot_params = jnp.zeros((3 * PP, SLOTS + LANES), F32)
        for i in range(4):
            nx, ny, nz = fn[0, i:i + 1, :], fn[1, i:i + 1, :], fn[2, i:i + 1, :]
            cw = speed * jnp.sqrt(nx * nx + ny * ny + nz * nz)
            rows = [0.5 * nx, 0.5 * ny, 0.5 * nz, cw]
            for j, row in enumerate(rows):
                fcoef[i, j] = spread(row)
            h = ori[i:i + 1, :]
            m0 = jnp.where(h == 0, 1.0, 0.0)
            m1 = jnp.where(h == 1, 1.0, 0.0)
            turn[i, 0] = spread(m0)
            turn[i, 1] = spread(m1)
            rows += [-lam, -2.0 * mu, -mu, -1.0 / rho, slip_scale, m0, m1]
            which = iota((PP, E), 0)
            block = jnp.zeros((PP, E), F32)
            for j, row in enumerate(rows):
                block = jnp.where(which == j, jnp.broadcast_to(row, (PP, E)), block)

            code = nc[i:i + 1, :]
            for j in range(4):
                p1[i, E * j:E * j + E, :] = jnp.where(iota((E, E), 0) + E * j == code, 1.0, 0.0).astype(BF16)
            halo = code - 1024
            number = jnp.zeros_like(halo)
            for m in range(1, 8):
                number = number + jnp.where(halo >= 28 * m, 1, 0)
            fault = code - 1248
            spot = jnp.where(fault >= 0, fault + SLOTS, jnp.where(halo >= 0, halo + 4 * number, -1))
            hot = jnp.where(iota((SLOTS + LANES, E), 0) == spot, 1.0, 0.0).astype(BF16)
            p2[i] = hot
            hi, rest = halves(block)
            mid, lo = halves(rest)
            left = jnp.concatenate([hi, mid, lo], axis=0).astype(BF16)
            slot_params = slot_params + lax.dot_general(
                left, hot, (((1,), (1,)), ((), ())), preferred_element_type=F32
            )
        slot_params = slot_params[0:PP] + slot_params[PP:2 * PP] + slot_params[2 * PP:3 * PP]
        for j in range(11):
            scoef[j] = jnp.broadcast_to(slot_params[j:j + 1, :], (8, SLOTS + LANES))

        fdip[...] = jnp.zeros_like(fdip)
        fdip[0:2, 0:FAULTS] = dip[...]
        polar, azimuth = fdip[0:1, :], fdip[1:2, :]
        fric[0] = jnp.broadcast_to(jnp.sin(polar) * jnp.cos(azimuth), (PP, LANES))
        fric[1] = jnp.broadcast_to(jnp.sin(polar) * jnp.sin(azimuth), (PP, LANES))
        fric[2] = jnp.broadcast_to(jnp.cos(polar), (PP, LANES))
        fric[3] = jnp.ones((PP, LANES), F32)
        fric[3, 0:PTS, 0:FAULTS] = coh[...]

    def split_modes(x):
        hi, lo = halves(x)
        return jnp.concatenate([hi, lo, hi, jnp.zeros((8, E), F32)], axis=0).astype(BF16)

    def sum_elastic(store):
        def body(rb, carry):
            def get(q, d):
                return R[q, pl.ds(pl.multiple_of(BP * d + 8 * rb, 8), 8), :]

            g = [[coef[3 * d + c] for c in range(3)] for d in range(3)]
            m = [coef[9 + j] for j in range(4)]
            grad = {}
            for i in range(3):
                v = [get(6 + i, d) for d in range(3)]
                for c in range(3):
                    grad[i, c] = v[0] * g[0][c] + v[1] * g[1][c] + v[2] * g[2][c]
            pressure = m[0] * (grad[0, 0] + grad[1, 1] + grad[2, 2])
            res = [
                pressure + m[1] * grad[0, 0],
                pressure + m[1] * grad[1, 1],
                pressure + m[1] * grad[2, 2],
                m[2] * (grad[0, 1] + grad[1, 0]),
                m[2] * (grad[1, 2] + grad[2, 1]),
                m[2] * (grad[0, 2] + grad[2, 0]),
            ]
            for kinds in ((0, 3, 5), (3, 1, 4), (5, 4, 2)):
                force = None
                for c, q in enumerate(kinds):
                    for d in range(3):
                        term = get(q, d) * g[d][c]
                        force = term if force is None else force + term
                res.append(m[3] * force)
            store(pl.ds(pl.multiple_of(8 * rb, 8), 8), res)
            return carry

        lax.fori_loop(0, BP // 8, body, 0, unroll=True)

    def send(step, k):
        return pltpu.make_async_remote_copy(
            src_ref=sendb.at[step, pl.ds(32 * k, 32)],
            dst_ref=recvb.at[step, pl.ds(32 * k, 32)],
            send_sem=send_sem.at[step, k],
            recv_sem=recv_sem.at[step, k],
            device_id=(me + OFFSETS[k], sub),
            device_id_type=MESH,
        )

    def send_fault(step):
        return pltpu.make_async_remote_copy(
            src_ref=sendf.at[step],
            dst_ref=recvf.at[step],
            send_sem=fsend_sem.at[step],
            recv_sem=frecv_sem.at[step],
            device_id=(me, partner),
            device_id_type=MESH,
        )

    def shifted(x, by):
        return jnp.concatenate(
            [pltpu.roll(x[:, LANES * t:LANES * t + LANES], by % LANES, 1) for t in range(SLOTS // LANES)], axis=1
        )

    in_block = iota((8, SLOTS), 1) & 31
    last_row = iota((8, SLOTS), 0) == 7

    def turned(x, first, second):
        r = fast_dot(lrot[...], jnp.concatenate([x[0], x[1], x[0]], axis=0))
        return jnp.where(first, r[0:PP], jnp.where(second, r[PP:2 * PP], r[2 * PP:3 * PP]))

    def slot_coefs(lanes):
        def double(j):
            return jnp.concatenate([scoef[j, :, lanes], scoef[j, :, lanes]], axis=0)

        return [double(j) for j in range(11)]

    def outer_flux(far, c):
        flux = elastic_rows(far, c[0:3], c[4:8])
        return [flux[q] - c[3] * far[q] for q in range(Q)]

    def stacked_rows(flux):
        parts = [halves(f) for f in flux]
        return jnp.concatenate([p[0] for p in parts] + [p[1] for p in parts], axis=0).astype(BF16)

    def update(step):
        factor = 1.0
        for degree in range(1, DEGREES + 1):
            source = state if degree == 1 else cur
            for q in range(Q):
                R[q] = fast_dot(lpred[...], split_modes(source[q]))
            factor = factor / (degree + 1)
            base = state if degree == 1 else integ

            def store(rows, res, factor=factor, base=base):
                for q in range(Q):
                    cur[q, rows, :] = res[q]
                    integ[q, rows, :] = base[q, rows, :] + factor * res[q]

            sum_elastic(store)

        for q in range(Q):
            t = fast_dot(lprj[...], split_modes(integ[q]))
            tr[q] = t
            hi, lo = both(t)
            for i in range(4):
                ths[PP * q:PP * q + PP, E * i:E * i + E] = hi[PP * i:PP * i + PP]
                ths[ROWS + PP * q:ROWS + PP * q + PP, E * i:E * i + E] = lo[PP * i:PP * i + PP]

        picked = fast_dot(ths[...], sp[...])
        picked = picked[0:ROWS] + picked[ROWS:2 * ROWS]
        tail = picked[128 + 8:ROWS]
        tiles = []
        for t in range(16):
            x = picked[8 * t:8 * t + 8]
            if t % 2 == 1:
                x = jnp.where(last_row, jnp.broadcast_to(picked[128 + t // 2:129 + t // 2], (8, SLOTS)), x)
            if t < 7:
                x = jnp.where(in_block >= 28, shifted(tail, 28 - 4 * t), x)
            tiles.append(x)
        sendb[step] = jnp.transpose(jnp.concatenate(tiles, axis=0))

        if step == 0:
            pl.semaphore_wait(barrier, 1 + jnp.minimum(me, 4) + jnp.minimum(n_dom - 1 - me, 4))

        for k in (3, 7, 2, 6, 1, 5, 0, 4):
            dst = me + OFFSETS[k]

            @pl.when((dst >= 0) & (dst < n_dom))
            def _():
                send(step, k).start()

        if step == 0:
            setup_fault()

        picked = fast_dot(ths[...], spf[...])
        sendf[step] = picked[0:ROWS] + picked[ROWS:2 * ROWS]
        send_fault(step).start()

        if step == 0:
            setup_rest()

        def own_face(i, c):
            g = fast_dot(ths[...], p1[i]).astype(BF16)
            m0, m1 = turn[i, 0] > 0.5, turn[i, 1] > 0.5
            for q in range(Q):
                hi = g[PP * q:PP * q + PP]
                lo = g[ROWS + PP * q:ROWS + PP * q + PP]
                r = fast_dot(lrot[...], jnp.concatenate([hi, lo, hi], axis=0))
                for half in range(2):
                    a = 8 * half
                    rt[q, pl.ds(pl.multiple_of(PP * i + a, 8), 8), :] = jnp.where(
                        m0, r[a:a + 8], jnp.where(m1, r[PP + a:PP + a + 8], r[2 * PP + a:2 * PP + a + 8])
                    )
            m = [coef[9 + j] for j in range(4)]
            n = [fcoef[i, j] for j in range(3)]
            cw = fcoef[i, 3]
            for half in range(2):
                rows = pl.ds(pl.multiple_of(PP * i + 8 * half, 8), 8)
                own = [tr[q, rows, :] for q in range(Q)]
                far = [rt[q, rows, :] for q in range(Q)]
                res = elastic_rows([x + y for x, y in zip(own, far)], n, m)
                for q in range(Q):
                    fx[q, rows, :] = res[q] + cw * (own[q] - far[q])
            return c

        lax.fori_loop(0, 4, own_face, 0, unroll=True)

        for q in range(Q):
            R[q] = fast_dot(lvol[...], split_modes(integ[q]))

        def store_volume(rows, res):
            for q in range(Q):
                cur[q, rows, :] = state[q, rows, :] + res[q]

        sum_elastic(store_volume)

        send_fault(step).wait_recv()
        c = slot_coefs(slice(SLOTS, SLOTS + LANES))
        first, second = c[9] > 0.5, c[10] > 0.5
        far = [turned(both(recvf[step, PP * q:PP * q + PP, :]), first, second) for q in range(Q)]
        flux = outer_flux(far, c)
        u = (fric[0], fric[1], fric[2])
        mean = [0.5 * (sendf[step, PP * q:PP * q + PP, :] + far[q]) for q in range(6)]
        force = traction(mean, u)
        along = force[0] * u[0] + force[1] * u[1] + force[2] * u[2]
        tangent = [force[a] - along * u[a] for a in range(3)]
        strength = fric[3] + FRICTION * jnp.maximum(-along, 0.0)
        size = jnp.sqrt(tangent[0] * tangent[0] + tangent[1] * tangent[1] + tangent[2] * tangent[2])
        over = 1.0 - strength / jnp.maximum(size, strength)
        for a in range(3):
            excess = over * tangent[a]
            flux[6 + a] = flux[6 + a] + excess * c[7]
            slipsum[PP * a:PP * a + PP, :] += excess * c[8]
        left = stacked_rows(flux)
        for i in range(4):
            r = fast_dot(left, p2[i, SLOTS:SLOTS + LANES, :])
            for q in range(Q):
                fx[q, PP * i:PP * i + PP, :] += r[PP * q:PP * q + PP] + r[ROWS + PP * q:ROWS + PP * q + PP]

        for q in range(Q):
            hi, lo = both(fx[q])
            lifted = fast_dot(llift[...], jnp.concatenate([hi, lo, hi], axis=0))
            cur[q] = cur[q] - lifted[0:BP]

        for k, o in enumerate(OFFSETS):
            src = me - o

            @pl.when((src >= 0) & (src < n_dom))
            def _():
                send(step, k).wait_recv()

        main = jnp.transpose(recvb[step])
        tail = jnp.zeros((8, SLOTS), F32)
        for t in range(7):
            tail = jnp.where((in_block >> 2) == t, shifted(main[8 * t:8 * t + 8], 4 * t - 28), tail)
        last = jnp.concatenate([main[PP * q + PTS:PP * q + PP] for q in range(8)] + [tail], axis=0)
        c = slot_coefs(slice(0, SLOTS))
        first, second = c[9] > 0.5, c[10] > 0.5
        far = [
            turned(both(main[PP * q:PP * q + PP] if q < 8 else last), first, second) for q in range(Q)
        ]
        left = stacked_rows(outer_flux(far, c))
        for i in range(4):
            hs[i] = fast_dot(left, p2[i, 0:SLOTS, :]).astype(BF16)
        for q in range(Q):
            his = [hs[i, PP * q:PP * q + PP, :] for i in range(4)]
            los = [hs[i, ROWS + PP * q:ROWS + PP * q + PP, :] for i in range(4)]
            lifted = fast_dot(llift[...], jnp.concatenate(his + los + his, axis=0))
            state[q] = cur[q] - lifted[0:BP]

    for step in range(STEPS):
        update(step)

    for q in range(Q):
        out[q] = state[q, 0:B, :]
    for a in range(3):
        slip[a] = slipsum[PP * a:PP * a + PTS, 0:FAULTS]

    for step in range(STEPS):
        for k, o in enumerate(OFFSETS):
            dst = me + o

            @pl.when((dst >= 0) & (dst < n_dom))
            def _():
                send(step, k).wait_send()

        send_fault(step).wait_send()


def on_device(n_dom, *args):
    (un, gr, fn, mat, live, nc, ori, sf, ff, dip, coh, st, pj, lf, ro) = args
    fn = jnp.transpose(fn, (1, 0, 2))
    pj = jnp.transpose(pj, (2, 0, 1))
    lf = jnp.transpose(lf, (1, 0, 2))
    args = (un, gr, fn, mat, nc, ori, sf.reshape(1, -1), ff.reshape(1, -1), dip, coh, st, pj, lf, ro)
    vmem = pl.BlockSpec(memory_space=pltpu.VMEM)
    args = [pltpu.with_memory_space_constraint(a, pltpu.HBM) for a in args]

    def f32(*shape):
        return pltpu.VMEM(shape, F32)

    def b16(*shape):
        return pltpu.VMEM(shape, BF16)

    updated, slip = pl.pallas_call(
        functools.partial(kernel, n_dom),
        out_shape=(
            jax.ShapeDtypeStruct((Q, B, E), F32),
            jax.ShapeDtypeStruct((3, PTS, FAULTS), F32),
        ),
        in_specs=[pl.BlockSpec(memory_space=pltpu.HBM)] * len(args),
        out_specs=(vmem, vmem),
        scratch_shapes=[pltpu.VMEM(a.shape, a.dtype) for a in args] + [
            f32(Q, BP, E),
            f32(Q, BP, E),
            f32(Q, BP, E),
            f32(Q, 128, E),
            f32(Q, 4 * PP, E),
            b16(2 * ROWS, 4 * E),
            f32(Q, 4 * PP, E),
            f32(Q, 4 * PP, E),
            b16(4, 4 * E, E),
            b16(4, SLOTS + LANES, E),
            b16(4 * E, SLOTS),
            b16(4 * E, LANES),
            b16(4, 2 * ROWS, E),
            f32(128, 128),
            f32(4 * PP, 128),
            b16(128, 128),
            b16(128, 128),
            b16(4 * PP, 128),
            b16(48, 12 * PP),
            b16(3 * PP, 3 * PP),
            f32(13, 8, E),
            f32(4, 4, 8, E),
            f32(4, 2, 8, E),
            f32(11, 8, SLOTS + LANES),
            pltpu.VMEM((8, LANES), jnp.int32),
            f32(8, LANES),
            f32(4, PP, LANES),
            f32(3 * PP, LANES),
            f32(STEPS, SLOTS, LANES),
            f32(STEPS, SLOTS, LANES),
            f32(STEPS, ROWS, LANES),
            f32(STEPS, ROWS, LANES),
            pltpu.SemaphoreType.DMA((len(args),)),
            pltpu.SemaphoreType.DMA((STEPS, 8)),
            pltpu.SemaphoreType.DMA((STEPS, 8)),
            pltpu.SemaphoreType.DMA((STEPS,)),
            pltpu.SemaphoreType.DMA((STEPS,)),
        ],
        compiler_params=pltpu.CompilerParams(
            collective_id=0, has_side_effects=True, vmem_limit_bytes=40 * 1024 * 1024
        ),
        name="ader_updates",
    )(*args)
    return jnp.where(iota((1, 1, E), 2) < live[0], updated, un), slip


def solution(mesh):
    split3 = P(None, None, ("dom", "sub"))
    split2 = P(None, ("dom", "sub"))
    split1 = P(("dom", "sub"))
    placed = (
        split3, split3, split3, split2, split1, split2, split2, split1, split1, split2, split2,
        P(), P(), P(), P(),
    )
    return jax.shard_map(
        functools.partial(on_device, mesh.shape["dom"]),
        mesh=mesh,
        in_specs=placed,
        out_specs=(split3, split3),
        check_vma=False,
    )
```

```python
import functools

import jax
import jax.numpy as jnp
from jax import lax
from jax.experimental import pallas as pl
from jax.experimental.pallas import tpu as pltpu
from jax.sharding import PartitionSpec as P

STEPS = 2
DEGREES = 4
OFFSETS = (1, 2, 3, 4, -1, -2, -3, -4)
FRICTION = 0.6
HIGHEST = lax.Precision.HIGHEST
MESH = pl.DeviceIdType.MESH

F32 = jnp.float32
BF16 = jnp.bfloat16
Q = 9
B = 35
BP = 40
PTS = 15
PP = 16
E = 256
SLOTS = 256
LANES = 128
FAULTS = 32
PARTS = 3
ROWS = Q * PP


def iota(shape, dim):
    return lax.broadcasted_iota(jnp.int32, shape, dim)


def exact_dot(a, b, dims=(((1,), (0,)), ((), ()))):
    return lax.dot_general(a, b, dims, precision=HIGHEST, preferred_element_type=F32)


def fast_dot(a, b, dims=(((1,), (0,)), ((), ()))):
    return lax.dot_general(a, b, dims, preferred_element_type=F32)


def halves(x):
    hi = x.astype(BF16).astype(F32)
    return hi, x - hi


def elastic_rows(s, n, m):
    px, py, pz = s[6] * n[0], s[7] * n[1], s[8] * n[2]
    pressure = m[0] * (px + py + pz)
    return (
        pressure + m[1] * px,
        pressure + m[1] * py,
        pressure + m[1] * pz,
        m[2] * (s[6] * n[1] + s[7] * n[0]),
        m[2] * (s[7] * n[2] + s[8] * n[1]),
        m[2] * (s[6] * n[2] + s[8] * n[0]),
        m[3] * (s[0] * n[0] + s[3] * n[1] + s[5] * n[2]),
        m[3] * (s[3] * n[0] + s[1] * n[1] + s[4] * n[2]),
        m[3] * (s[5] * n[0] + s[4] * n[1] + s[2] * n[2]),
    )


def traction(s, n):
    return (
        s[0] * n[0] + s[3] * n[1] + s[5] * n[2],
        s[3] * n[0] + s[1] * n[1] + s[4] * n[2],
        s[5] * n[0] + s[4] * n[1] + s[2] * n[2],
    )


def kernel(
    n_dom,
    un_hbm, gr_hbm, fn_hbm, mat_hbm, nc_hbm, ori_hbm, sf_hbm, ff_hbm, dip_hbm, coh_hbm,
    st_hbm, pj_hbm, lf_hbm, ro_hbm,
    out, slip,
    un, gr, fn, mat, nc, ori, sf, ff, dip, coh, st, pj, lf, ro,
    state, cur, integ, R, tr, ths, rt, fx, p1, p2, sp, spf, hs,
    pull, drive, lsf, lsp, lforce, lpred, lvol, lprj, llift, lrot, coef, fcoef, turn, scoef, fcode, fdip, fric, slipsum,
    sendb, recvb, sgf, sendf, recvf,
    in_sem, send_sem, recv_sem, fsend_sem, frecv_sem,
):
    me = lax.axis_index("dom")
    sub = lax.axis_index("sub")
    partner = sub + 1 - 2 * (sub % 2)

    sources = (st_hbm, un_hbm, gr_hbm, mat_hbm, sf_hbm, pj_hbm, ff_hbm, nc_hbm, fn_hbm, ori_hbm,
               dip_hbm, coh_hbm, lf_hbm, ro_hbm)
    targets = (st, un, gr, mat, sf, pj, ff, nc, fn, ori, dip, coh, lf, ro)
    loads = [pltpu.make_async_copy(a, b, in_sem.at[j]) for j, (a, b) in enumerate(zip(sources, targets))]
    for load in loads:
        load.start()

    barrier = pltpu.get_barrier_semaphore()
    for o in OFFSETS:
        dst = me + o

        @pl.when((dst >= 0) & (dst < n_dom))
        def _():
            pl.semaphore_signal(barrier, inc=1, device_id=(dst, sub), device_id_type=MESH)

    pl.semaphore_signal(barrier, inc=1, device_id=(me, partner), device_id_type=MESH)

    for k, o in enumerate(OFFSETS):
        src = me - o

        @pl.when((src < 0) | (src >= n_dom))
        def _():
            for step in range(STEPS):
                recvb[step, 32 * k:32 * k + 32, :] = jnp.zeros((32, 128), F32)

    rep = (iota((B, 128), 0) == iota((B, 128), 1) % BP) & (iota((B, 128), 1) < 3 * BP)
    low_part = iota((B, 128), 1) >= 2 * BP
    rep_hi = jnp.where(rep & ~low_part, 1.0, 0.0).astype(BF16)
    rep_lo = jnp.where(rep & low_part, 1.0, 0.0).astype(BF16)
    row, col = iota((2 * BP, 128), 0), iota((2 * BP, 128), 1)
    rep2 = (row % BP == col % BP) & (row % BP < B) & (col < 3 * BP) & ((row >= BP) == (col >= 2 * BP))
    rep2 = jnp.where(rep2, 1.0, 0.0).astype(BF16)
    TN = (((0,), (0,)), ((), ()))

    def stacked(x, low):
        hi, lo = halves(x)
        return jnp.where(low, lo, hi).astype(BF16)

    def both(x):
        hi, lo = halves(x)
        return hi.astype(BF16), lo.astype(BF16)

    def stack_low(x):
        hi, lo = halves(jnp.concatenate([x, jnp.zeros((BP - B, x.shape[1]), F32)], axis=0))
        return jnp.concatenate([hi, lo], axis=0).astype(BF16)

    def spread(row):
        return jnp.broadcast_to(row, (8, E))

    place_h = jnp.where(
        ((iota((224, SLOTS), 1) & 31) < 28)
        & (iota((224, SLOTS), 0) == 28 * (iota((224, SLOTS), 1) >> 5) + (iota((224, SLOTS), 1) & 31)),
        1.0, 0.0,
    )
    unused = (iota((1, SLOTS), 1) & 31) >= 28
    lsf[...] = jnp.zeros_like(lsf)
    slipsum[...] = jnp.zeros_like(slipsum)

    for load in loads[0:6]:
        load.wait()
    for d in range(3):
        lsf[BP * d:BP * d + B, :] = fast_dot(stack_low(st[d]), rep2, TN)
    lpred[...] = lsf[...].astype(BF16)
    row, col = iota((2 * BP, 384), 0), iota((2 * BP, 384), 1)
    total = jnp.zeros((B, 384), F32)
    for d in range(3):
        inner = col - 3 * BP * d
        hot = (row % BP == col % BP) & (row % BP < B) & (inner >= 0) & (inner < 3 * BP)
        hot = jnp.where(hot & ((row >= BP) == (inner >= 2 * BP)), 1.0, 0.0).astype(BF16)
        total = total + fast_dot(stack_low(st[d]), hot, TN)
    lforce[...] = jnp.concatenate([total, jnp.zeros((48 - B, 384), F32)], axis=0).astype(BF16)

    for q in range(Q):
        state[q] = jnp.concatenate([un[q], jnp.zeros((BP - B, E), F32)], axis=0)
    for d in range(3):
        for c in range(3):
            coef[3 * d + c] = spread(gr[d, c:c + 1, :])
    lam, mu, rho = mat[0:1, :], mat[1:2, :], mat[2:3, :]
    for j, row in enumerate((-lam, -2.0 * mu, -mu, -1.0 / rho)):
        coef[9 + j] = spread(row)

    raw = jnp.broadcast_to(sf[...], (8, 224))
    raw = jnp.concatenate([raw >> 8, raw & 255], axis=0).astype(F32).astype(BF16)
    placed = fast_dot(raw, place_h.astype(BF16))
    codes = (placed[0:1, :] * 256.0 + placed[8:9, :] + 0.5).astype(jnp.int32)
    codes = jnp.where(unused, -1, codes)
    for i in range(4):
        sp[E * i:E * i + E, :] = jnp.where(iota((E, SLOTS), 0) + E * i == codes, 1.0, 0.0).astype(BF16)
    lsp[...] = jnp.zeros_like(lsp)
    for i in range(4):
        hi, lo = both(pj[:, i, :])
        lsp[PP * i:PP * i + PTS, :] = fast_dot(hi, rep_hi) + fast_dot(lo, rep_lo)
    lprj[...] = lsp[...].astype(BF16)

    def setup_fault():
        loads[6].wait()
        fcode[...] = jnp.full(fcode.shape, -1, jnp.int32)
        fcode[0:1, 0:FAULTS] = ff[...]
        for i in range(4):
            hot = iota((E, LANES), 0) + E * i == fcode[0:1, :]
            spf[E * i:E * i + E, :] = jnp.where(hot, 1.0, 0.0).astype(BF16)

    def setup_rest():
        for load in loads[7:]:
            load.wait()
        for d in range(3):
            hi, lo = both(st[d])
            lsf[BP * d:BP * d + B, :] = fast_dot(hi, rep_hi) + fast_dot(lo, rep_lo)
        lvol[...] = lsf[...].astype(BF16)
        total = jnp.zeros((B, 12 * PP), F32)
        for i in range(4):
            place = iota((PTS, 12 * PP), 1) % (4 * PP) == iota((PTS, 12 * PP), 0) + PP * i
            total = total + exact_dot(lf[:, i, :], jnp.where(place, 1.0, 0.0), TN)
        total = jnp.concatenate([total, jnp.zeros((48 - B, 12 * PP), F32)], axis=0)
        llift[...] = stacked(total, iota((48, 12 * PP), 1) >= 8 * PP)
        place = jnp.where(iota((PTS, 3 * PP), 1) % PP == iota((PTS, 3 * PP), 0), 1.0, 0.0)
        pad = jnp.zeros((PP - PTS, 3 * PP), F32)
        turns = []
        for h in range(3):
            turns += [exact_dot(ro[h], place, TN), pad]
        lrot[...] = stacked(jnp.concatenate(turns, axis=0), iota((3 * PP, 3 * PP), 1) >= 2 * PP)

        lam, mu, rho = mat[0:1, :], mat[1:2, :], mat[2:3, :]
        speed = 0.5 * jnp.sqrt((lam + 2.0 * mu) / rho)
        slip_scale = 1.0 / jnp.sqrt(mu * rho)
        slot_params = jnp.zeros((3 * PP, SLOTS + LANES), F32)
        for i in range(4):
            nx, ny, nz = fn[0, i:i + 1, :], fn[1, i:i + 1, :], fn[2, i:i + 1, :]
            cw = speed * jnp.sqrt(nx * nx + ny * ny + nz * nz)
            rows = [0.5 * nx, 0.5 * ny, 0.5 * nz, cw]
            for j, row in enumerate(rows):
                fcoef[i, j] = spread(row)
            h = ori[i:i + 1, :]
            m0 = jnp.where(h == 0, 1.0, 0.0)
            m1 = jnp.where(h == 1, 1.0, 0.0)
            turn[i, 0] = spread(m0)
            turn[i, 1] = spread(m1)
            rows += [-lam, -2.0 * mu, -mu, -1.0 / rho, slip_scale, m0, m1]
            which = iota((PP, E), 0)
            block = jnp.zeros((PP, E), F32)
            for j, row in enumerate(rows):
                block = jnp.where(which == j, jnp.broadcast_to(row, (PP, E)), block)

            code = nc[i:i + 1, :]
            for j in range(4):
                p1[i, E * j:E * j + E, :] = jnp.where(iota((E, E), 0) + E * j == code, 1.0, 0.0).astype(BF16)
            halo = code - 1024
            number = jnp.zeros_like(halo)
            for m in range(1, 8):
                number = number + jnp.where(halo >= 28 * m, 1, 0)
            fault = code - 1248
            spot = jnp.where(fault >= 0, fault + SLOTS, jnp.where(halo >= 0, halo + 4 * number, -1))
            hot = jnp.where(iota((SLOTS + LANES, E), 0) == spot, 1.0, 0.0).astype(BF16)
            p2[i] = hot
            hi, rest = halves(block)
            mid, lo = halves(rest)
            left = jnp.concatenate([hi, mid, lo], axis=0).astype(BF16)
            slot_params = slot_params + lax.dot_general(
                left, hot, (((1,), (1,)), ((), ())), preferred_element_type=F32
            )
        slot_params = slot_params[0:PP] + slot_params[PP:2 * PP] + slot_params[2 * PP:3 * PP]
        for j in range(11):
            scoef[j] = jnp.broadcast_to(slot_params[j:j + 1, :], (8, SLOTS + LANES))

        fdip[...] = jnp.zeros_like(fdip)
        fdip[0:2, 0:FAULTS] = dip[...]
        polar, azimuth = fdip[0:1, :], fdip[1:2, :]
        fric[0] = jnp.broadcast_to(jnp.sin(polar) * jnp.cos(azimuth), (PP, LANES))
        fric[1] = jnp.broadcast_to(jnp.sin(polar) * jnp.sin(azimuth), (PP, LANES))
        fric[2] = jnp.broadcast_to(jnp.cos(polar), (PP, LANES))
        fric[3] = jnp.ones((PP, LANES), F32)
        fric[3, 0:PTS, 0:FAULTS] = coh[...]

    def split_modes(x):
        hi, lo = halves(x)
        return jnp.concatenate([hi, lo, hi, jnp.zeros((8, E), F32)], axis=0).astype(BF16)

    def sum_elastic(store):
        def body(rb, carry):
            def get(q, d):
                return R[q, pl.ds(pl.multiple_of(BP * d + 8 * rb, 8), 8), :]

            g = [[coef[3 * d + c] for c in range(3)] for d in range(3)]
            m = [coef[9 + j] for j in range(4)]
            grad = {}
            for i in range(3):
                v = [get(6 + i, d) for d in range(3)]
                for c in range(3):
                    grad[i, c] = v[0] * g[0][c] + v[1] * g[1][c] + v[2] * g[2][c]
            pressure = m[0] * (grad[0, 0] + grad[1, 1] + grad[2, 2])
            res = [
                pressure + m[1] * grad[0, 0],
                pressure + m[1] * grad[1, 1],
                pressure + m[1] * grad[2, 2],
                m[2] * (grad[0, 1] + grad[1, 0]),
                m[2] * (grad[1, 2] + grad[2, 1]),
                m[2] * (grad[0, 2] + grad[2, 0]),
            ]
            for kinds in ((0, 3, 5), (3, 1, 4), (5, 4, 2)):
                force = None
                for c, q in enumerate(kinds):
                    for d in range(3):
                        term = get(q, d) * g[d][c]
                        force = term if force is None else force + term
                res.append(m[3] * force)
            store(pl.ds(pl.multiple_of(8 * rb, 8), 8), res)
            return carry

        lax.fori_loop(0, BP // 8, body, 0, unroll=True)

    def send(step, k):
        return pltpu.make_async_remote_copy(
            src_ref=sendb.at[step, pl.ds(32 * k, 32)],
            dst_ref=recvb.at[step, pl.ds(32 * k, 32)],
            send_sem=send_sem.at[step, k],
            recv_sem=recv_sem.at[step, k],
            device_id=(me + OFFSETS[k], sub),
            device_id_type=MESH,
        )

    def send_fault(step):
        return pltpu.make_async_remote_copy(
            src_ref=sendf.at[step],
            dst_ref=recvf.at[step],
            send_sem=fsend_sem.at[step],
            recv_sem=frecv_sem.at[step],
            device_id=(me, partner),
            device_id_type=MESH,
        )

    def shifted(x, by):
        return jnp.concatenate(
            [pltpu.roll(x[:, LANES * t:LANES * t + LANES], by % LANES, 1) for t in range(SLOTS // LANES)], axis=1
        )

    in_block = iota((8, SLOTS), 1) & 31
    last_row = iota((8, SLOTS), 0) == 7

    def turned(x, first, second):
        r = fast_dot(lrot[...], jnp.concatenate([x[0], x[1], x[0]], axis=0))
        return jnp.where(first, r[0:PP], jnp.where(second, r[PP:2 * PP], r[2 * PP:3 * PP]))

    def slot_coefs(lanes):
        def double(j):
            return jnp.concatenate([scoef[j, :, lanes], scoef[j, :, lanes]], axis=0)

        return [double(j) for j in range(11)]

    def outer_flux(far, c):
        flux = elastic_rows(far, c[0:3], c[4:8])
        return [flux[q] - c[3] * far[q] for q in range(Q)]

    def stacked_rows(flux):
        parts = [halves(f) for f in flux]
        return jnp.concatenate([p[0] for p in parts] + [p[1] for p in parts], axis=0).astype(BF16)

    def update(step):
        def forces(rows, sigma):
            g = [[coef[3 * d + c] for c in range(3)] for d in range(3)]
            for c, kinds in enumerate(((0, 3, 5), (3, 1, 4), (5, 4, 2))):
                for d in range(3):
                    pull[3 * c + d, rows, :] = (
                        sigma[kinds[0]] * g[d][0] + sigma[kinds[1]] * g[d][1] + sigma[kinds[2]] * g[d][2]
                    )

        def first(rb, carry):
            rows = pl.ds(pl.multiple_of(8 * rb, 8), 8)
            forces(rows, [state[q, rows, :] for q in range(6)])
            return carry

        lax.fori_loop(0, BP // 8, first, 0, unroll=True)
        factor = 1.0
        for degree in range(1, DEGREES + 1):
            for i in range(3):
                x = state[6 + i] if degree == 1 else cur[6 + i]
                R[i] = fast_dot(lpred[...], split_modes(x))
            for c in range(3):
                pieces = []
                for d in range(3):
                    hi, lo = halves(pull[3 * c + d])
                    pieces += [hi, lo, hi]
                pieces = jnp.concatenate(pieces + [jnp.zeros((24, E), F32)], axis=0).astype(BF16)
                drive[c] = fast_dot(lforce[...], pieces)
            factor = factor / (degree + 1)

            def body(rb, carry, factor=factor, degree=degree):
                rows = pl.ds(pl.multiple_of(8 * rb, 8), 8)
                g = [[coef[3 * d + c] for c in range(3)] for d in range(3)]
                m = [coef[9 + j] for j in range(4)]
                grad = {}
                for i in range(3):
                    v = [R[i, pl.ds(pl.multiple_of(BP * d + 8 * rb, 8), 8), :] for d in range(3)]
                    for c in range(3):
                        grad[i, c] = v[0] * g[0][c] + v[1] * g[1][c] + v[2] * g[2][c]
                pressure = m[0] * (grad[0, 0] + grad[1, 1] + grad[2, 2])
                res = [
                    pressure + m[1] * grad[0, 0],
                    pressure + m[1] * grad[1, 1],
                    pressure + m[1] * grad[2, 2],
                    m[2] * (grad[0, 1] + grad[1, 0]),
                    m[2] * (grad[1, 2] + grad[2, 1]),
                    m[2] * (grad[0, 2] + grad[2, 0]),
                ]
                res += [m[3] * drive[c, rows, :] for c in range(3)]
                base = state if degree == 1 else integ
                for q in range(Q):
                    integ[q, rows, :] = base[q, rows, :] + factor * res[q]
                if degree < DEGREES:
                    for i in range(3):
                        cur[6 + i, rows, :] = res[6 + i]
                    forces(rows, res[0:6])
                return carry

            lax.fori_loop(0, BP // 8, body, 0, unroll=True)

        for q in range(Q):
            t = fast_dot(lprj[...], split_modes(integ[q]))
            tr[q] = t
            hi, lo = both(t)
            for i in range(4):
                ths[PP * q:PP * q + PP, E * i:E * i + E] = hi[PP * i:PP * i + PP]
                ths[ROWS + PP * q:ROWS + PP * q + PP, E * i:E * i + E] = lo[PP * i:PP * i + PP]

        picked = fast_dot(ths[...], sp[...])
        picked = picked[0:ROWS] + picked[ROWS:2 * ROWS]
        tail = picked[128 + 8:ROWS]
        tiles = []
        for t in range(16):
            x = picked[8 * t:8 * t + 8]
            if t % 2 == 1:
                x = jnp.where(last_row, jnp.broadcast_to(picked[128 + t // 2:129 + t // 2], (8, SLOTS)), x)
            if t < 7:
                x = jnp.where(in_block >= 28, shifted(tail, 28 - 4 * t), x)
            tiles.append(x)
        sendb[step] = jnp.transpose(jnp.concatenate(tiles, axis=0))

        if step == 0:
            pl.semaphore_wait(barrier, 1 + jnp.minimum(me, 4) + jnp.minimum(n_dom - 1 - me, 4))

        for k in (3, 7, 2, 6, 1, 5, 0, 4):
            dst = me + OFFSETS[k]

            @pl.when((dst >= 0) & (dst < n_dom))
            def _():
                send(step, k).start()

        if step == 0:
            setup_fault()

        picked = fast_dot(ths[...], spf[...])
        picked = picked[0:ROWS] + picked[ROWS:2 * ROWS]
        sgf[...] = picked
        sendf[step] = (
            picked[0:3 * PP]
            + pltpu.roll(picked[3 * PP:6 * PP], FAULTS, 1)
            + pltpu.roll(picked[6 * PP:9 * PP], 2 * FAULTS, 1)
        )
        send_fault(step).start()

        if step == 0:
            setup_rest()

        def own_face(i, c):
            g = fast_dot(ths[...], p1[i]).astype(BF16)
            m0, m1 = turn[i, 0] > 0.5, turn[i, 1] > 0.5
            for q in range(Q):
                hi = g[PP * q:PP * q + PP]
                lo = g[ROWS + PP * q:ROWS + PP * q + PP]
                r = fast_dot(lrot[...], jnp.concatenate([hi, lo, hi], axis=0))
                for half in range(2):
                    a = 8 * half
                    rt[q, pl.ds(pl.multiple_of(PP * i + a, 8), 8), :] = jnp.where(
                        m0, r[a:a + 8], jnp.where(m1, r[PP + a:PP + a + 8], r[2 * PP + a:2 * PP + a + 8])
                    )
            m = [coef[9 + j] for j in range(4)]
            n = [fcoef[i, j] for j in range(3)]
            cw = fcoef[i, 3]
            for half in range(2):
                rows = pl.ds(pl.multiple_of(PP * i + 8 * half, 8), 8)
                own = [tr[q, rows, :] for q in range(Q)]
                far = [rt[q, rows, :] for q in range(Q)]
                res = elastic_rows([x + y for x, y in zip(own, far)], n, m)
                for q in range(Q):
                    fx[q, rows, :] = res[q] + cw * (own[q] - far[q])
            return c

        lax.fori_loop(0, 4, own_face, 0, unroll=True)

        for q in range(Q):
            R[q] = fast_dot(lvol[...], split_modes(integ[q]))

        def store_volume(rows, res):
            for q in range(Q):
                cur[q, rows, :] = state[q, rows, :] + res[q]

        sum_elastic(store_volume)

        send_fault(step).wait_recv()
        c = slot_coefs(slice(SLOTS, SLOTS + LANES))
        first, second = c[9] > 0.5, c[10] > 0.5
        came = recvf[step]
        came = [came, pltpu.roll(came, LANES - FAULTS, 1), pltpu.roll(came, LANES - 2 * FAULTS, 1)]
        came = jnp.concatenate(came, axis=0)
        far = [turned(both(came[PP * q:PP * q + PP]), first, second) for q in range(Q)]
        flux = outer_flux(far, c)
        u = (fric[0], fric[1], fric[2])
        mean = [0.5 * (sgf[PP * q:PP * q + PP, :] + far[q]) for q in range(6)]
        force = traction(mean, u)
        along = force[0] * u[0] + force[1] * u[1] + force[2] * u[2]
        tangent = [force[a] - along * u[a] for a in range(3)]
        strength = fric[3] + FRICTION * jnp.maximum(-along, 0.0)
        size = jnp.sqrt(tangent[0] * tangent[0] + tangent[1] * tangent[1] + tangent[2] * tangent[2])
        over = 1.0 - strength / jnp.maximum(size, strength)
        for a in range(3):
            excess = over * tangent[a]
            flux[6 + a] = flux[6 + a] + excess * c[7]
            slipsum[PP * a:PP * a + PP, :] += excess * c[8]
        left = stacked_rows(flux)
        for i in range(4):
            r = fast_dot(left, p2[i, SLOTS:SLOTS + LANES, :])
            for q in range(Q):
                fx[q, PP * i:PP * i + PP, :] += r[PP * q:PP * q + PP] + r[ROWS + PP * q:ROWS + PP * q + PP]

        for q in range(Q):
            hi, lo = both(fx[q])
            lifted = fast_dot(llift[...], jnp.concatenate([hi, lo, hi], axis=0))
            cur[q] = cur[q] - lifted[0:BP]

        for k, o in enumerate(OFFSETS):
            src = me - o

            @pl.when((src >= 0) & (src < n_dom))
            def _():
                send(step, k).wait_recv()

        main = jnp.transpose(recvb[step])
        tail = jnp.zeros((8, SLOTS), F32)
        for t in range(7):
            tail = jnp.where((in_block >> 2) == t, shifted(main[8 * t:8 * t + 8], 4 * t - 28), tail)
        last = jnp.concatenate([main[PP * q + PTS:PP * q + PP] for q in range(8)] + [tail], axis=0)
        c = slot_coefs(slice(0, SLOTS))
        first, second = c[9] > 0.5, c[10] > 0.5
        far = [
            turned(both(main[PP * q:PP * q + PP] if q < 8 else last), first, second) for q in range(Q)
        ]
        left = stacked_rows(outer_flux(far, c))
        for i in range(4):
            hs[i] = fast_dot(left, p2[i, 0:SLOTS, :]).astype(BF16)
        for q in range(Q):
            his = [hs[i, PP * q:PP * q + PP, :] for i in range(4)]
            los = [hs[i, ROWS + PP * q:ROWS + PP * q + PP, :] for i in range(4)]
            lifted = fast_dot(llift[...], jnp.concatenate(his + los + his, axis=0))
            state[q] = cur[q] - lifted[0:BP]

    for step in range(STEPS):
        update(step)

    for q in range(Q):
        out[q] = state[q, 0:B, :]
    for a in range(3):
        slip[a] = slipsum[PP * a:PP * a + PTS, 0:FAULTS]

    for step in range(STEPS):
        for k, o in enumerate(OFFSETS):
            dst = me + o

            @pl.when((dst >= 0) & (dst < n_dom))
            def _():
                send(step, k).wait_send()

        send_fault(step).wait_send()


def select_live(live, un, updated, slip, out_hbm, slip_hbm, out, sem):
    copies = [pltpu.make_async_copy(slip, slip_hbm, sem.at[PARTS])]
    copies[0].start()
    alive = jnp.broadcast_to(iota((1, E), 1) < live[0:1, 0:1], (B, E))
    size = Q // PARTS
    for part in range(PARTS):
        for q in range(part * size, part * size + size):
            out[q] = jnp.where(alive, updated[q], un[q])
        rows = pl.ds(part * size, size)
        copies.append(pltpu.make_async_copy(out.at[rows], out_hbm.at[rows], sem.at[part]))
        copies[-1].start()
    for copy in copies:
        copy.wait()


def on_device(n_dom, *args):
    (un, gr, fn, mat, live, nc, ori, sf, ff, dip, coh, st, pj, lf, ro) = args
    fn = jnp.transpose(fn, (1, 0, 2))
    pj = jnp.transpose(pj, (2, 0, 1))
    lf = jnp.transpose(lf, (1, 0, 2))
    args = (un, gr, fn, mat, nc, ori, sf.reshape(1, -1), ff.reshape(1, -1), dip, coh, st, pj, lf, ro)
    vmem = pl.BlockSpec(memory_space=pltpu.VMEM)
    args = [pltpu.with_memory_space_constraint(a, pltpu.HBM) for a in args]

    def f32(*shape):
        return pltpu.VMEM(shape, F32)

    def b16(*shape):
        return pltpu.VMEM(shape, BF16)

    updated, slip = pl.pallas_call(
        functools.partial(kernel, n_dom),
        out_shape=(
            jax.ShapeDtypeStruct((Q, B, E), F32),
            jax.ShapeDtypeStruct((3, PTS, FAULTS), F32),
        ),
        in_specs=[pl.BlockSpec(memory_space=pltpu.HBM)] * len(args),
        out_specs=(vmem, vmem),
        scratch_shapes=[pltpu.VMEM(a.shape, a.dtype) for a in args] + [
            f32(Q, BP, E),
            f32(Q, BP, E),
            f32(Q, BP, E),
            f32(Q, 128, E),
            f32(Q, 4 * PP, E),
            b16(2 * ROWS, 4 * E),
            f32(Q, 4 * PP, E),
            f32(Q, 4 * PP, E),
            b16(4, 4 * E, E),
            b16(4, SLOTS + LANES, E),
            b16(4 * E, SLOTS),
            b16(4 * E, LANES),
            b16(4, 2 * ROWS, E),
            f32(Q, BP, E),
            f32(3, 48, E),
            f32(128, 128),
            f32(4 * PP, 128),
            b16(48, 384),
            b16(128, 128),
            b16(128, 128),
            b16(4 * PP, 128),
            b16(48, 12 * PP),
            b16(3 * PP, 3 * PP),
            f32(13, 8, E),
            f32(4, 4, 8, E),
            f32(4, 2, 8, E),
            f32(11, 8, SLOTS + LANES),
            pltpu.VMEM((8, LANES), jnp.int32),
            f32(8, LANES),
            f32(4, PP, LANES),
            f32(3 * PP, LANES),
            f32(STEPS, SLOTS, LANES),
            f32(STEPS, SLOTS, LANES),
            f32(ROWS, LANES),
            f32(STEPS, 3 * PP, LANES),
            f32(STEPS, 3 * PP, LANES),
            pltpu.SemaphoreType.DMA((len(args),)),
            pltpu.SemaphoreType.DMA((STEPS, 8)),
            pltpu.SemaphoreType.DMA((STEPS, 8)),
            pltpu.SemaphoreType.DMA((STEPS,)),
            pltpu.SemaphoreType.DMA((STEPS,)),
        ],
        compiler_params=pltpu.CompilerParams(
            collective_id=0, has_side_effects=True, vmem_limit_bytes=40 * 1024 * 1024
        ),
        name="ader_updates",
    )(*args)
    live = lax.pad(live, jnp.int32(0), ((0, LANES - 1, 0),)).reshape(1, LANES)
    hbm = pl.BlockSpec(memory_space=pl.ANY)
    return pl.pallas_call(
        select_live,
        out_shape=(
            jax.ShapeDtypeStruct((Q, B, E), F32),
            jax.ShapeDtypeStruct((3, PTS, FAULTS), F32),
        ),
        in_specs=[vmem] * 4,
        out_specs=(hbm, hbm),
        scratch_shapes=[f32(Q, B, E), pltpu.SemaphoreType.DMA((PARTS + 1,))],
        compiler_params=pltpu.CompilerParams(vmem_limit_bytes=4 * 1024 * 1024),
        name="select_live",
    )(live, un, updated, slip)


def solution(mesh):
    split3 = P(None, None, ("dom", "sub"))
    split2 = P(None, ("dom", "sub"))
    split1 = P(("dom", "sub"))
    placed = (
        split3, split3, split3, split2, split1, split2, split2, split1, split1, split2, split2,
        P(), P(), P(), P(),
    )
    return jax.shard_map(
        functools.partial(on_device, mesh.shape["dom"]),
        mesh=mesh,
        in_specs=placed,
        out_specs=(split3, split3),
        check_vma=False,
    )
```

```python
import functools

import jax
import jax.numpy as jnp
from jax import lax
from jax.experimental import pallas as pl
from jax.experimental.pallas import tpu as pltpu
from jax.sharding import PartitionSpec as P

STEPS = 2
DEGREES = 4
OFFSETS = (1, 2, 3, 4, -1, -2, -3, -4)
FRICTION = 0.6
HIGHEST = lax.Precision.HIGHEST
MESH = pl.DeviceIdType.MESH

F32 = jnp.float32
BF16 = jnp.bfloat16
Q = 9
B = 35
BP = 40
PTS = 15
PP = 16
E = 256
SLOTS = 256
LANES = 128
FAULTS = 32
PARTS = 3
ROWS = Q * PP


def iota(shape, dim):
    return lax.broadcasted_iota(jnp.int32, shape, dim)


def exact_dot(a, b, dims=(((1,), (0,)), ((), ()))):
    return lax.dot_general(a, b, dims, precision=HIGHEST, preferred_element_type=F32)


def fast_dot(a, b, dims=(((1,), (0,)), ((), ()))):
    return lax.dot_general(a, b, dims, preferred_element_type=F32)


def halves(x):
    hi = x.astype(BF16).astype(F32)
    return hi, x - hi


def elastic_rows(s, n, m):
    px, py, pz = s[6] * n[0], s[7] * n[1], s[8] * n[2]
    pressure = m[0] * (px + py + pz)
    return (
        pressure + m[1] * px,
        pressure + m[1] * py,
        pressure + m[1] * pz,
        m[2] * (s[6] * n[1] + s[7] * n[0]),
        m[2] * (s[7] * n[2] + s[8] * n[1]),
        m[2] * (s[6] * n[2] + s[8] * n[0]),
        m[3] * (s[0] * n[0] + s[3] * n[1] + s[5] * n[2]),
        m[3] * (s[3] * n[0] + s[1] * n[1] + s[4] * n[2]),
        m[3] * (s[5] * n[0] + s[4] * n[1] + s[2] * n[2]),
    )


def traction(s, n):
    return (
        s[0] * n[0] + s[3] * n[1] + s[5] * n[2],
        s[3] * n[0] + s[1] * n[1] + s[4] * n[2],
        s[5] * n[0] + s[4] * n[1] + s[2] * n[2],
    )


def kernel(
    n_dom,
    un_hbm, gr_hbm, fn_hbm, mat_hbm, nc_hbm, ori_hbm, sf_hbm, ff_hbm, dip_hbm, coh_hbm,
    st_hbm, pj_hbm, lf_hbm, ro_hbm,
    out, slip,
    un, gr, fn, mat, nc, ori, sf, ff, dip, coh, st, pj, lf, ro,
    state, cur, integ, R, tr, ths, rt, fx, p1, p2, sp, spf, hs,
    pull, drive, lsf, lsp, lforce, lpred, lvol, lprj, llift, lrot, coef, fcoef, turn, scoef, fcode, fdip, fric, slipsum,
    sendb, recvb, sgf, sendf, recvf,
    in_sem, send_sem, recv_sem, fsend_sem, frecv_sem,
):
    me = lax.axis_index("dom")
    sub = lax.axis_index("sub")
    partner = sub + 1 - 2 * (sub % 2)

    sources = (st_hbm, un_hbm, gr_hbm, mat_hbm, sf_hbm, pj_hbm, ff_hbm, nc_hbm, fn_hbm, ori_hbm,
               dip_hbm, coh_hbm, lf_hbm, ro_hbm)
    targets = (st, un, gr, mat, sf, pj, ff, nc, fn, ori, dip, coh, lf, ro)
    loads = [pltpu.make_async_copy(a, b, in_sem.at[j]) for j, (a, b) in enumerate(zip(sources, targets))]
    for load in loads:
        load.start()

    barrier = pltpu.get_barrier_semaphore()
    for o in OFFSETS:
        dst = me + o

        @pl.when((dst >= 0) & (dst < n_dom))
        def _():
            pl.semaphore_signal(barrier, inc=1, device_id=(dst, sub), device_id_type=MESH)

    pl.semaphore_signal(barrier, inc=1, device_id=(me, partner), device_id_type=MESH)

    for k, o in enumerate(OFFSETS):
        src = me - o

        @pl.when((src < 0) | (src >= n_dom))
        def _():
            for step in range(STEPS):
                recvb[step, 32 * k:32 * k + 32, :] = jnp.zeros((32, 128), F32)

    rep = (iota((B, 128), 0) == iota((B, 128), 1) % BP) & (iota((B, 128), 1) < 3 * BP)
    low_part = iota((B, 128), 1) >= 2 * BP
    rep_hi = jnp.where(rep & ~low_part, 1.0, 0.0).astype(BF16)
    rep_lo = jnp.where(rep & low_part, 1.0, 0.0).astype(BF16)
    row, col = iota((2 * BP, 128), 0), iota((2 * BP, 128), 1)
    rep2 = (row % BP == col % BP) & (row % BP < B) & (col < 3 * BP) & ((row >= BP) == (col >= 2 * BP))
    rep2 = jnp.where(rep2, 1.0, 0.0).astype(BF16)
    TN = (((0,), (0,)), ((), ()))

    def stacked(x, low):
        hi, lo = halves(x)
        return jnp.where(low, lo, hi).astype(BF16)

    def both(x):
        hi, lo = halves(x)
        return hi.astype(BF16), lo.astype(BF16)

    def stack_low(x):
        hi, lo = halves(jnp.concatenate([x, jnp.zeros((BP - B, x.shape[1]), F32)], axis=0))
        return jnp.concatenate([hi, lo], axis=0).astype(BF16)

    def spread(row):
        return jnp.broadcast_to(row, (8, E))

    place_h = jnp.where(
        ((iota((224, SLOTS), 1) & 31) < 28)
        & (iota((224, SLOTS), 0) == 28 * (iota((224, SLOTS), 1) >> 5) + (iota((224, SLOTS), 1) & 31)),
        1.0, 0.0,
    )
    unused = (iota((1, SLOTS), 1) & 31) >= 28
    lsf[...] = jnp.zeros_like(lsf)
    slipsum[...] = jnp.zeros_like(slipsum)

    for load in loads[0:6]:
        load.wait()
    for d in range(3):
        lsf[BP * d:BP * d + B, :] = fast_dot(stack_low(st[d]), rep2, TN)
    lpred[...] = lsf[...].astype(BF16)
    row, col = iota((2 * BP, 384), 0), iota((2 * BP, 384), 1)
    total = jnp.zeros((B, 384), F32)
    for d in range(3):
        inner = col - 3 * BP * d
        hot = (row % BP == col % BP) & (row % BP < B) & (inner >= 0) & (inner < 3 * BP)
        hot = jnp.where(hot & ((row >= BP) == (inner >= 2 * BP)), 1.0, 0.0).astype(BF16)
        total = total + fast_dot(stack_low(st[d]), hot, TN)
    lforce[...] = jnp.concatenate([total, jnp.zeros((48 - B, 384), F32)], axis=0).astype(BF16)

    for q in range(Q):
        state[q] = jnp.concatenate([un[q], jnp.zeros((BP - B, E), F32)], axis=0)
    for d in range(3):
        for c in range(3):
            coef[3 * d + c] = spread(gr[d, c:c + 1, :])
    lam, mu, rho = mat[0:1, :], mat[1:2, :], mat[2:3, :]
    for j, row in enumerate((-lam, -2.0 * mu, -mu, -1.0 / rho)):
        coef[9 + j] = spread(row)

    raw = jnp.broadcast_to(sf[...], (8, 224))
    raw = jnp.concatenate([raw >> 8, raw & 255], axis=0).astype(F32).astype(BF16)
    placed = fast_dot(raw, place_h.astype(BF16))
    codes = (placed[0:1, :] * 256.0 + placed[8:9, :] + 0.5).astype(jnp.int32)
    codes = jnp.where(unused, -1, codes)
    for i in range(4):
        sp[E * i:E * i + E, :] = jnp.where(iota((E, SLOTS), 0) + E * i == codes, 1.0, 0.0).astype(BF16)
    lsp[...] = jnp.zeros_like(lsp)
    for i in range(4):
        hi, lo = both(pj[:, i, :])
        lsp[PP * i:PP * i + PTS, :] = fast_dot(hi, rep_hi) + fast_dot(lo, rep_lo)
    lprj[...] = lsp[...].astype(BF16)

    def setup_fault():
        loads[6].wait()
        fcode[...] = jnp.full(fcode.shape, -1, jnp.int32)
        fcode[0:1, 0:FAULTS] = ff[...]
        for i in range(4):
            hot = iota((E, LANES), 0) + E * i == fcode[0:1, :]
            spf[E * i:E * i + E, :] = jnp.where(hot, 1.0, 0.0).astype(BF16)

    def setup_rest():
        for load in loads[7:]:
            load.wait()
        for d in range(3):
            hi, lo = both(st[d])
            lsf[BP * d:BP * d + B, :] = fast_dot(hi, rep_hi) + fast_dot(lo, rep_lo)
        lvol[...] = lsf[...].astype(BF16)
        total = jnp.zeros((B, 12 * PP), F32)
        for i in range(4):
            place = iota((PTS, 12 * PP), 1) % (4 * PP) == iota((PTS, 12 * PP), 0) + PP * i
            total = total + exact_dot(lf[:, i, :], jnp.where(place, 1.0, 0.0), TN)
        total = jnp.concatenate([total, jnp.zeros((48 - B, 12 * PP), F32)], axis=0)
        llift[...] = stacked(total, iota((48, 12 * PP), 1) >= 8 * PP)
        place = jnp.where(iota((PTS, 3 * PP), 1) % PP == iota((PTS, 3 * PP), 0), 1.0, 0.0)
        pad = jnp.zeros((PP - PTS, 3 * PP), F32)
        turns = []
        for h in range(3):
            turns += [exact_dot(ro[h], place, TN), pad]
        lrot[...] = stacked(jnp.concatenate(turns, axis=0), iota((3 * PP, 3 * PP), 1) >= 2 * PP)

        lam, mu, rho = mat[0:1, :], mat[1:2, :], mat[2:3, :]
        speed = 0.5 * jnp.sqrt((lam + 2.0 * mu) / rho)
        slip_scale = 1.0 / jnp.sqrt(mu * rho)
        slot_params = jnp.zeros((3 * PP, SLOTS + LANES), F32)
        for i in range(4):
            nx, ny, nz = fn[0, i:i + 1, :], fn[1, i:i + 1, :], fn[2, i:i + 1, :]
            cw = speed * jnp.sqrt(nx * nx + ny * ny + nz * nz)
            rows = [0.5 * nx, 0.5 * ny, 0.5 * nz, cw]
            for j, row in enumerate(rows):
                fcoef[i, j] = spread(row)
            h = ori[i:i + 1, :]
            m0 = jnp.where(h == 0, 1.0, 0.0)
            m1 = jnp.where(h == 1, 1.0, 0.0)
            turn[i, 0] = spread(m0)
            turn[i, 1] = spread(m1)
            rows += [-lam, -2.0 * mu, -mu, -1.0 / rho, slip_scale, m0, m1]
            which = iota((PP, E), 0)
            block = jnp.zeros((PP, E), F32)
            for j, row in enumerate(rows):
                block = jnp.where(which == j, jnp.broadcast_to(row, (PP, E)), block)

            code = nc[i:i + 1, :]
            for j in range(4):
                p1[i, E * j:E * j + E, :] = jnp.where(iota((E, E), 0) + E * j == code, 1.0, 0.0).astype(BF16)
            halo = code - 1024
            number = jnp.zeros_like(halo)
            for m in range(1, 8):
                number = number + jnp.where(halo >= 28 * m, 1, 0)
            fault = code - 1248
            spot = jnp.where(fault >= 0, fault + SLOTS, jnp.where(halo >= 0, halo + 4 * number, -1))
            hot = jnp.where(iota((SLOTS + LANES, E), 0) == spot, 1.0, 0.0).astype(BF16)
            p2[i] = hot
            hi, rest = halves(block)
            mid, lo = halves(rest)
            left = jnp.concatenate([hi, mid, lo], axis=0).astype(BF16)
            slot_params = slot_params + lax.dot_general(
                left, hot, (((1,), (1,)), ((), ())), preferred_element_type=F32
            )
        slot_params = slot_params[0:PP] + slot_params[PP:2 * PP] + slot_params[2 * PP:3 * PP]
        for j in range(11):
            scoef[j] = jnp.broadcast_to(slot_params[j:j + 1, :], (8, SLOTS + LANES))

        fdip[...] = jnp.zeros_like(fdip)
        fdip[0:2, 0:FAULTS] = dip[...]
        polar, azimuth = fdip[0:1, :], fdip[1:2, :]
        fric[0] = jnp.broadcast_to(jnp.sin(polar) * jnp.cos(azimuth), (PP, LANES))
        fric[1] = jnp.broadcast_to(jnp.sin(polar) * jnp.sin(azimuth), (PP, LANES))
        fric[2] = jnp.broadcast_to(jnp.cos(polar), (PP, LANES))
        fric[3] = jnp.ones((PP, LANES), F32)
        fric[3, 0:PTS, 0:FAULTS] = coh[...]

    def split_modes(x):
        hi, lo = halves(x)
        return jnp.concatenate([hi, lo, hi, jnp.zeros((8, E), F32)], axis=0).astype(BF16)

    def sum_elastic(store):
        def body(rb, carry):
            def get(q, d):
                return R[q, pl.ds(pl.multiple_of(BP * d + 8 * rb, 8), 8), :]

            g = [[coef[3 * d + c] for c in range(3)] for d in range(3)]
            m = [coef[9 + j] for j in range(4)]
            grad = {}
            for i in range(3):
                v = [get(6 + i, d) for d in range(3)]
                for c in range(3):
                    grad[i, c] = v[0] * g[0][c] + v[1] * g[1][c] + v[2] * g[2][c]
            pressure = m[0] * (grad[0, 0] + grad[1, 1] + grad[2, 2])
            res = [
                pressure + m[1] * grad[0, 0],
                pressure + m[1] * grad[1, 1],
                pressure + m[1] * grad[2, 2],
                m[2] * (grad[0, 1] + grad[1, 0]),
                m[2] * (grad[1, 2] + grad[2, 1]),
                m[2] * (grad[0, 2] + grad[2, 0]),
            ]
            for kinds in ((0, 3, 5), (3, 1, 4), (5, 4, 2)):
                force = None
                for c, q in enumerate(kinds):
                    for d in range(3):
                        term = get(q, d) * g[d][c]
                        force = term if force is None else force + term
                res.append(m[3] * force)
            store(pl.ds(pl.multiple_of(8 * rb, 8), 8), res)
            return carry

        lax.fori_loop(0, BP // 8, body, 0, unroll=True)

    def send(step, k):
        return pltpu.make_async_remote_copy(
            src_ref=sendb.at[step, pl.ds(32 * k, 32)],
            dst_ref=recvb.at[step, pl.ds(32 * k, 32)],
            send_sem=send_sem.at[step, k],
            recv_sem=recv_sem.at[step, k],
            device_id=(me + OFFSETS[k], sub),
            device_id_type=MESH,
        )

    def send_fault(step):
        return pltpu.make_async_remote_copy(
            src_ref=sendf.at[step],
            dst_ref=recvf.at[step],
            send_sem=fsend_sem.at[step],
            recv_sem=frecv_sem.at[step],
            device_id=(me, partner),
            device_id_type=MESH,
        )

    def shifted(x, by):
        return jnp.concatenate(
            [pltpu.roll(x[:, LANES * t:LANES * t + LANES], by % LANES, 1) for t in range(SLOTS // LANES)], axis=1
        )

    in_block = iota((8, SLOTS), 1) & 31
    last_row = iota((8, SLOTS), 0) == 7

    def turned(x, first, second):
        r = fast_dot(lrot[...], jnp.concatenate([x[0], x[1], x[0]], axis=0))
        return jnp.where(first, r[0:PP], jnp.where(second, r[PP:2 * PP], r[2 * PP:3 * PP]))

    def slot_coefs(lanes):
        def double(j):
            return jnp.concatenate([scoef[j, :, lanes], scoef[j, :, lanes]], axis=0)

        return [double(j) for j in range(11)]

    def outer_flux(far, c):
        flux = elastic_rows(far, c[0:3], c[4:8])
        return [flux[q] - c[3] * far[q] for q in range(Q)]

    def stacked_rows(flux):
        parts = [halves(f) for f in flux]
        return jnp.concatenate([p[0] for p in parts] + [p[1] for p in parts], axis=0).astype(BF16)

    def update(step):
        def forces(rows, sigma):
            g = [[coef[3 * d + c] for c in range(3)] for d in range(3)]
            for c, kinds in enumerate(((0, 3, 5), (3, 1, 4), (5, 4, 2))):
                for d in range(3):
                    pull[3 * c + d, rows, :] = (
                        sigma[kinds[0]] * g[d][0] + sigma[kinds[1]] * g[d][1] + sigma[kinds[2]] * g[d][2]
                    )

        def first(rb, carry):
            rows = pl.ds(pl.multiple_of(8 * rb, 8), 8)
            forces(rows, [state[q, rows, :] for q in range(6)])
            return carry

        lax.fori_loop(0, BP // 8, first, 0, unroll=True)
        factor = 1.0
        for degree in range(1, DEGREES + 1):
            for i in range(3):
                x = state[6 + i] if degree == 1 else cur[6 + i]
                R[i] = fast_dot(lpred[...], split_modes(x))
            for c in range(3):
                pieces = []
                for d in range(3):
                    hi, lo = halves(pull[3 * c + d])
                    pieces += [hi, lo, hi]
                pieces = jnp.concatenate(pieces + [jnp.zeros((24, E), F32)], axis=0).astype(BF16)
                drive[c] = fast_dot(lforce[...], pieces)
            factor = factor / (degree + 1)

            def body(rb, carry, factor=factor, degree=degree):
                rows = pl.ds(pl.multiple_of(8 * rb, 8), 8)
                g = [[coef[3 * d + c] for c in range(3)] for d in range(3)]
                m = [coef[9 + j] for j in range(4)]
                grad = {}
                for i in range(3):
                    v = [R[i, pl.ds(pl.multiple_of(BP * d + 8 * rb, 8), 8), :] for d in range(3)]
                    for c in range(3):
                        grad[i, c] = v[0] * g[0][c] + v[1] * g[1][c] + v[2] * g[2][c]
                pressure = m[0] * (grad[0, 0] + grad[1, 1] + grad[2, 2])
                res = [
                    pressure + m[1] * grad[0, 0],
                    pressure + m[1] * grad[1, 1],
                    pressure + m[1] * grad[2, 2],
                    m[2] * (grad[0, 1] + grad[1, 0]),
                    m[2] * (grad[1, 2] + grad[2, 1]),
                    m[2] * (grad[0, 2] + grad[2, 0]),
                ]
                res += [m[3] * drive[c, rows, :] for c in range(3)]
                base = state if degree == 1 else integ
                for q in range(Q):
                    integ[q, rows, :] = base[q, rows, :] + factor * res[q]
                if degree < DEGREES:
                    for i in range(3):
                        cur[6 + i, rows, :] = res[6 + i]
                    forces(rows, res[0:6])
                return carry

            lax.fori_loop(0, BP // 8, body, 0, unroll=True)

        for q in range(Q):
            t = fast_dot(lprj[...], split_modes(integ[q]))
            tr[q] = t
            hi, lo = both(t)
            for i in range(4):
                ths[PP * q:PP * q + PP, E * i:E * i + E] = hi[PP * i:PP * i + PP]
                ths[ROWS + PP * q:ROWS + PP * q + PP, E * i:E * i + E] = lo[PP * i:PP * i + PP]

        picked = fast_dot(ths[...], sp[...])
        picked = picked[0:ROWS] + picked[ROWS:2 * ROWS]
        tail = picked[128 + 8:ROWS]
        tiles = []
        for t in range(16):
            x = picked[8 * t:8 * t + 8]
            if t % 2 == 1:
                x = jnp.where(last_row, jnp.broadcast_to(picked[128 + t // 2:129 + t // 2], (8, SLOTS)), x)
            if t < 7:
                x = jnp.where(in_block >= 28, shifted(tail, 28 - 4 * t), x)
            tiles.append(x)
        sendb[step] = jnp.transpose(jnp.concatenate(tiles, axis=0))

        if step == 0:
            pl.semaphore_wait(barrier, 1 + jnp.minimum(me, 4) + jnp.minimum(n_dom - 1 - me, 4))

        for k in (3, 7, 2, 6, 1, 5, 0, 4):
            dst = me + OFFSETS[k]

            @pl.when((dst >= 0) & (dst < n_dom))
            def _():
                send(step, k).start()

        if step == 0:
            setup_fault()

        picked = fast_dot(ths[...], spf[...])
        picked = picked[0:ROWS] + picked[ROWS:2 * ROWS]
        sgf[...] = picked
        sendf[step] = (
            picked[0:3 * PP]
            + pltpu.roll(picked[3 * PP:6 * PP], FAULTS, 1)
            + pltpu.roll(picked[6 * PP:9 * PP], 2 * FAULTS, 1)
        )
        send_fault(step).start()

        if step == 0:
            setup_rest()

        def own_face(i, c):
            g = fast_dot(ths[...], p1[i]).astype(BF16)
            m0, m1 = turn[i, 0] > 0.5, turn[i, 1] > 0.5
            for q in range(Q):
                hi = g[PP * q:PP * q + PP]
                lo = g[ROWS + PP * q:ROWS + PP * q + PP]
                r = fast_dot(lrot[...], jnp.concatenate([hi, lo, hi], axis=0))
                for half in range(2):
                    a = 8 * half
                    rt[q, pl.ds(pl.multiple_of(PP * i + a, 8), 8), :] = jnp.where(
                        m0, r[a:a + 8], jnp.where(m1, r[PP + a:PP + a + 8], r[2 * PP + a:2 * PP + a + 8])
                    )
            m = [coef[9 + j] for j in range(4)]
            n = [fcoef[i, j] for j in range(3)]
            cw = fcoef[i, 3]
            for half in range(2):
                rows = pl.ds(pl.multiple_of(PP * i + 8 * half, 8), 8)
                own = [tr[q, rows, :] for q in range(Q)]
                far = [rt[q, rows, :] for q in range(Q)]
                res = elastic_rows([x + y for x, y in zip(own, far)], n, m)
                for q in range(Q):
                    fx[q, rows, :] = res[q] + cw * (own[q] - far[q])
            return c

        lax.fori_loop(0, 4, own_face, 0, unroll=True)

        for q in range(Q):
            R[q] = fast_dot(lvol[...], split_modes(integ[q]))

        def store_volume(rows, res):
            for q in range(Q):
                cur[q, rows, :] = state[q, rows, :] + res[q]

        sum_elastic(store_volume)

        send_fault(step).wait_recv()
        c = slot_coefs(slice(SLOTS, SLOTS + LANES))
        first, second = c[9] > 0.5, c[10] > 0.5
        came = recvf[step]
        came = [came, pltpu.roll(came, LANES - FAULTS, 1), pltpu.roll(came, LANES - 2 * FAULTS, 1)]
        came = jnp.concatenate(came, axis=0)
        far = [turned(both(came[PP * q:PP * q + PP]), first, second) for q in range(Q)]
        flux = outer_flux(far, c)
        u = (fric[0], fric[1], fric[2])
        mean = [0.5 * (sgf[PP * q:PP * q + PP, :] + far[q]) for q in range(6)]
        force = traction(mean, u)
        along = force[0] * u[0] + force[1] * u[1] + force[2] * u[2]
        tangent = [force[a] - along * u[a] for a in range(3)]
        strength = fric[3] + FRICTION * jnp.maximum(-along, 0.0)
        size = jnp.sqrt(tangent[0] * tangent[0] + tangent[1] * tangent[1] + tangent[2] * tangent[2])
        over = 1.0 - strength / jnp.maximum(size, strength)
        for a in range(3):
            excess = over * tangent[a]
            flux[6 + a] = flux[6 + a] + excess * c[7]
            slipsum[PP * a:PP * a + PP, :] += excess * c[8]
        left = stacked_rows(flux)
        for i in range(4):
            r = fast_dot(left, p2[i, SLOTS:SLOTS + LANES, :])
            for q in range(Q):
                fx[q, PP * i:PP * i + PP, :] += r[PP * q:PP * q + PP] + r[ROWS + PP * q:ROWS + PP * q + PP]

        for q in range(Q):
            hi, lo = both(fx[q])
            lifted = fast_dot(llift[...], jnp.concatenate([hi, lo, hi], axis=0))
            cur[q] = cur[q] - lifted[0:BP]

        for k, o in enumerate(OFFSETS):
            dst = me + o

            @pl.when((dst >= 0) & (dst < n_dom))
            def _():
                send(step, k).wait_send()

        send_fault(step).wait_send()

        for k in (0, 4, 1, 5, 2, 6, 3, 7):
            src = me - OFFSETS[k]

            @pl.when((src >= 0) & (src < n_dom))
            def _():
                send(step, k).wait_recv()

        main = jnp.transpose(recvb[step])
        tail = jnp.zeros((8, SLOTS), F32)
        for t in range(7):
            tail = jnp.where((in_block >> 2) == t, shifted(main[8 * t:8 * t + 8], 4 * t - 28), tail)
        last = jnp.concatenate([main[PP * q + PTS:PP * q + PP] for q in range(8)] + [tail], axis=0)
        c = slot_coefs(slice(0, SLOTS))
        first, second = c[9] > 0.5, c[10] > 0.5
        far = [
            turned(both(main[PP * q:PP * q + PP] if q < 8 else last), first, second) for q in range(Q)
        ]
        left = stacked_rows(outer_flux(far, c))
        for i in range(4):
            hs[i] = fast_dot(left, p2[i, 0:SLOTS, :]).astype(BF16)
        for q in range(Q):
            his = [hs[i, PP * q:PP * q + PP, :] for i in range(4)]
            los = [hs[i, ROWS + PP * q:ROWS + PP * q + PP, :] for i in range(4)]
            lifted = fast_dot(llift[...], jnp.concatenate(his + los + his, axis=0))
            if step < STEPS - 1:
                state[q] = cur[q] - lifted[0:BP]
            else:
                out[q] = cur[q, 0:B, :] - lifted[0:B]

    for step in range(STEPS):
        update(step)

    for a in range(3):
        slip[a] = slipsum[PP * a:PP * a + PTS, 0:FAULTS]


def select_live(live, un, updated, slip, out_hbm, slip_hbm, out, sem):
    copies = [pltpu.make_async_copy(slip, slip_hbm, sem.at[PARTS])]
    copies[0].start()
    alive = jnp.broadcast_to(iota((1, E), 1) < live[0:1, 0:1], (B, E))
    size = Q // PARTS
    for part in range(PARTS):
        for q in range(part * size, part * size + size):
            out[q] = jnp.where(alive, updated[q], un[q])
        rows = pl.ds(part * size, size)
        copies.append(pltpu.make_async_copy(out.at[rows], out_hbm.at[rows], sem.at[part]))
        copies[-1].start()
    for copy in copies:
        copy.wait()


def on_device(n_dom, *args):
    (un, gr, fn, mat, live, nc, ori, sf, ff, dip, coh, st, pj, lf, ro) = args
    fn = jnp.transpose(fn, (1, 0, 2))
    pj = jnp.transpose(pj, (2, 0, 1))
    lf = jnp.transpose(lf, (1, 0, 2))
    args = (un, gr, fn, mat, nc, ori, sf.reshape(1, -1), ff.reshape(1, -1), dip, coh, st, pj, lf, ro)
    vmem = pl.BlockSpec(memory_space=pltpu.VMEM)
    args = [pltpu.with_memory_space_constraint(a, pltpu.HBM) for a in args]

    def f32(*shape):
        return pltpu.VMEM(shape, F32)

    def b16(*shape):
        return pltpu.VMEM(shape, BF16)

    updated, slip = pl.pallas_call(
        functools.partial(kernel, n_dom),
        out_shape=(
            jax.ShapeDtypeStruct((Q, B, E), F32),
            jax.ShapeDtypeStruct((3, PTS, FAULTS), F32),
        ),
        in_specs=[pl.BlockSpec(memory_space=pltpu.HBM)] * len(args),
        out_specs=(vmem, vmem),
        scratch_shapes=[pltpu.VMEM(a.shape, a.dtype) for a in args] + [
            f32(Q, BP, E),
            f32(Q, BP, E),
            f32(Q, BP, E),
            f32(Q, 128, E),
            f32(Q, 4 * PP, E),
            b16(2 * ROWS, 4 * E),
            f32(Q, 4 * PP, E),
            f32(Q, 4 * PP, E),
            b16(4, 4 * E, E),
            b16(4, SLOTS + LANES, E),
            b16(4 * E, SLOTS),
            b16(4 * E, LANES),
            b16(4, 2 * ROWS, E),
            f32(Q, BP, E),
            f32(3, 48, E),
            f32(128, 128),
            f32(4 * PP, 128),
            b16(48, 384),
            b16(128, 128),
            b16(128, 128),
            b16(4 * PP, 128),
            b16(48, 12 * PP),
            b16(3 * PP, 3 * PP),
            f32(13, 8, E),
            f32(4, 4, 8, E),
            f32(4, 2, 8, E),
            f32(11, 8, SLOTS + LANES),
            pltpu.VMEM((8, LANES), jnp.int32),
            f32(8, LANES),
            f32(4, PP, LANES),
            f32(3 * PP, LANES),
            f32(STEPS, SLOTS, LANES),
            f32(STEPS, SLOTS, LANES),
            f32(ROWS, LANES),
            f32(STEPS, 3 * PP, LANES),
            f32(STEPS, 3 * PP, LANES),
            pltpu.SemaphoreType.DMA((len(args),)),
            pltpu.SemaphoreType.DMA((STEPS, 8)),
            pltpu.SemaphoreType.DMA((STEPS, 8)),
            pltpu.SemaphoreType.DMA((STEPS,)),
            pltpu.SemaphoreType.DMA((STEPS,)),
        ],
        compiler_params=pltpu.CompilerParams(
            collective_id=0, has_side_effects=True, vmem_limit_bytes=40 * 1024 * 1024
        ),
        name="ader_updates",
    )(*args)
    live = lax.pad(live, jnp.int32(0), ((0, LANES - 1, 0),)).reshape(1, LANES)
    hbm = pl.BlockSpec(memory_space=pl.ANY)
    return pl.pallas_call(
        select_live,
        out_shape=(
            jax.ShapeDtypeStruct((Q, B, E), F32),
            jax.ShapeDtypeStruct((3, PTS, FAULTS), F32),
        ),
        in_specs=[vmem] * 4,
        out_specs=(hbm, hbm),
        scratch_shapes=[f32(Q, B, E), pltpu.SemaphoreType.DMA((PARTS + 1,))],
        compiler_params=pltpu.CompilerParams(vmem_limit_bytes=4 * 1024 * 1024),
        name="select_live",
    )(live, un, updated, slip)


def solution(mesh):
    split3 = P(None, None, ("dom", "sub"))
    split2 = P(None, ("dom", "sub"))
    split1 = P(("dom", "sub"))
    placed = (
        split3, split3, split3, split2, split1, split2, split2, split1, split1, split2, split2,
        P(), P(), P(), P(),
    )
    return jax.shard_map(
        functools.partial(on_device, mesh.shape["dom"]),
        mesh=mesh,
        in_specs=placed,
        out_specs=(split3, split3),
        check_vma=False,
    )
```

```python
import functools

import jax
import jax.numpy as jnp
from jax import lax
from jax.experimental import pallas as pl
from jax.experimental.pallas import tpu as pltpu
from jax.sharding import PartitionSpec as P

STEPS = 2
DEGREES = 4
OFFSETS = (1, 2, 3, 4, -1, -2, -3, -4)
FRICTION = 0.6
HIGHEST = lax.Precision.HIGHEST
MESH = pl.DeviceIdType.MESH

F32 = jnp.float32
BF16 = jnp.bfloat16
Q = 9
B = 35
BP = 40
PTS = 15
PP = 16
E = 256
SLOTS = 256
LANES = 128
FAULTS = 32
PARTS = 3
ROWS = Q * PP


def iota(shape, dim):
    return lax.broadcasted_iota(jnp.int32, shape, dim)


def exact_dot(a, b, dims=(((1,), (0,)), ((), ()))):
    return lax.dot_general(a, b, dims, precision=HIGHEST, preferred_element_type=F32)


def fast_dot(a, b, dims=(((1,), (0,)), ((), ()))):
    return lax.dot_general(a, b, dims, preferred_element_type=F32)


def halves(x):
    hi = x.astype(BF16).astype(F32)
    return hi, x - hi


def elastic_rows(s, n, m):
    px, py, pz = s[6] * n[0], s[7] * n[1], s[8] * n[2]
    pressure = m[0] * (px + py + pz)
    return (
        pressure + m[1] * px,
        pressure + m[1] * py,
        pressure + m[1] * pz,
        m[2] * (s[6] * n[1] + s[7] * n[0]),
        m[2] * (s[7] * n[2] + s[8] * n[1]),
        m[2] * (s[6] * n[2] + s[8] * n[0]),
        m[3] * (s[0] * n[0] + s[3] * n[1] + s[5] * n[2]),
        m[3] * (s[3] * n[0] + s[1] * n[1] + s[4] * n[2]),
        m[3] * (s[5] * n[0] + s[4] * n[1] + s[2] * n[2]),
    )


def traction(s, n):
    return (
        s[0] * n[0] + s[3] * n[1] + s[5] * n[2],
        s[3] * n[0] + s[1] * n[1] + s[4] * n[2],
        s[5] * n[0] + s[4] * n[1] + s[2] * n[2],
    )


def kernel(
    n_dom,
    un_hbm, gr_hbm, fn_hbm, mat_hbm, nc_hbm, ori_hbm, sf_hbm, ff_hbm, dip_hbm, coh_hbm,
    st_hbm, pj_hbm, lf_hbm, ro_hbm,
    out, slip,
    un, gr, fn, mat, nc, ori, sf, ff, dip, coh, st, pj, lf, ro,
    state, cur, integ, R, tr, ths, rt, fx, p1, p2, sp, spf, hs,
    pull, drive, lsf, lsp, lforce, lpred, lvol, lprj, llift, lrot, coef, fcoef, turn, scoef, fcode, fdip, fric, slipsum,
    sendb, recvb, sgf, sendf, recvf,
    in_sem, send_sem, recv_sem, fsend_sem, frecv_sem,
):
    me = lax.axis_index("dom")
    sub = lax.axis_index("sub")
    partner = sub + 1 - 2 * (sub % 2)
    inside = (me >= 4) & (me < n_dom - 4)

    sources = (st_hbm, un_hbm, gr_hbm, mat_hbm, sf_hbm, pj_hbm, ff_hbm, nc_hbm, fn_hbm, ori_hbm,
               dip_hbm, coh_hbm, lf_hbm, ro_hbm)
    targets = (st, un, gr, mat, sf, pj, ff, nc, fn, ori, dip, coh, lf, ro)
    loads = [pltpu.make_async_copy(a, b, in_sem.at[j]) for j, (a, b) in enumerate(zip(sources, targets))]
    for load in loads:
        load.start()

    barrier = pltpu.get_barrier_semaphore()
    for o in OFFSETS:
        dst = me + o

        @pl.when((dst >= 0) & (dst < n_dom))
        def _():
            pl.semaphore_signal(barrier, inc=1, device_id=(dst, sub), device_id_type=MESH)

    pl.semaphore_signal(barrier, inc=1, device_id=(me, partner), device_id_type=MESH)

    for k, o in enumerate(OFFSETS):
        src = me - o

        @pl.when((src < 0) | (src >= n_dom))
        def _():
            for step in range(STEPS):
                recvb[step, 32 * k:32 * k + 32, :] = jnp.zeros((32, 128), F32)

    rep = (iota((B, 128), 0) == iota((B, 128), 1) % BP) & (iota((B, 128), 1) < 3 * BP)
    low_part = iota((B, 128), 1) >= 2 * BP
    rep_hi = jnp.where(rep & ~low_part, 1.0, 0.0).astype(BF16)
    rep_lo = jnp.where(rep & low_part, 1.0, 0.0).astype(BF16)
    row, col = iota((2 * BP, 128), 0), iota((2 * BP, 128), 1)
    rep2 = (row % BP == col % BP) & (row % BP < B) & (col < 3 * BP) & ((row >= BP) == (col >= 2 * BP))
    rep2 = jnp.where(rep2, 1.0, 0.0).astype(BF16)
    TN = (((0,), (0,)), ((), ()))

    def stacked(x, low):
        hi, lo = halves(x)
        return jnp.where(low, lo, hi).astype(BF16)

    def both(x):
        hi, lo = halves(x)
        return hi.astype(BF16), lo.astype(BF16)

    def stack_low(x):
        hi, lo = halves(jnp.concatenate([x, jnp.zeros((BP - B, x.shape[1]), F32)], axis=0))
        return jnp.concatenate([hi, lo], axis=0).astype(BF16)

    def spread(row):
        return jnp.broadcast_to(row, (8, E))

    place_h = jnp.where(
        ((iota((224, SLOTS), 1) & 31) < 28)
        & (iota((224, SLOTS), 0) == 28 * (iota((224, SLOTS), 1) >> 5) + (iota((224, SLOTS), 1) & 31)),
        1.0, 0.0,
    )
    unused = (iota((1, SLOTS), 1) & 31) >= 28
    lsf[...] = jnp.zeros_like(lsf)
    slipsum[...] = jnp.zeros_like(slipsum)

    for load in loads[0:6]:
        load.wait()
    for d in range(3):
        lsf[BP * d:BP * d + B, :] = fast_dot(stack_low(st[d]), rep2, TN)
    lpred[...] = lsf[...].astype(BF16)
    row, col = iota((2 * BP, 384), 0), iota((2 * BP, 384), 1)
    total = jnp.zeros((B, 384), F32)
    for d in range(3):
        inner = col - 3 * BP * d
        hot = (row % BP == col % BP) & (row % BP < B) & (inner >= 0) & (inner < 3 * BP)
        hot = jnp.where(hot & ((row >= BP) == (inner >= 2 * BP)), 1.0, 0.0).astype(BF16)
        total = total + fast_dot(stack_low(st[d]), hot, TN)
    lforce[...] = jnp.concatenate([total, jnp.zeros((48 - B, 384), F32)], axis=0).astype(BF16)

    for q in range(Q):
        state[q] = jnp.concatenate([un[q], jnp.zeros((BP - B, E), F32)], axis=0)
    for d in range(3):
        for c in range(3):
            coef[3 * d + c] = spread(gr[d, c:c + 1, :])
    lam, mu, rho = mat[0:1, :], mat[1:2, :], mat[2:3, :]
    for j, row in enumerate((-lam, -2.0 * mu, -mu, -1.0 / rho)):
        coef[9 + j] = spread(row)

    raw = jnp.broadcast_to(sf[...], (8, 224))
    raw = jnp.concatenate([raw >> 8, raw & 255], axis=0).astype(F32).astype(BF16)
    placed = fast_dot(raw, place_h.astype(BF16))
    codes = (placed[0:1, :] * 256.0 + placed[8:9, :] + 0.5).astype(jnp.int32)
    codes = jnp.where(unused, -1, codes)
    for i in range(4):
        sp[E * i:E * i + E, :] = jnp.where(iota((E, SLOTS), 0) + E * i == codes, 1.0, 0.0).astype(BF16)
    lsp[...] = jnp.zeros_like(lsp)
    for i in range(4):
        hi, lo = both(pj[:, i, :])
        lsp[PP * i:PP * i + PTS, :] = fast_dot(hi, rep_hi) + fast_dot(lo, rep_lo)
    lprj[...] = lsp[...].astype(BF16)

    def setup_fault():
        loads[6].wait()
        fcode[...] = jnp.full(fcode.shape, -1, jnp.int32)
        fcode[0:1, 0:FAULTS] = ff[...]
        for i in range(4):
            hot = iota((E, LANES), 0) + E * i == fcode[0:1, :]
            spf[E * i:E * i + E, :] = jnp.where(hot, 1.0, 0.0).astype(BF16)

    def setup_rest():
        for load in loads[7:]:
            load.wait()
        for d in range(3):
            hi, lo = both(st[d])
            lsf[BP * d:BP * d + B, :] = fast_dot(hi, rep_hi) + fast_dot(lo, rep_lo)
        lvol[...] = lsf[...].astype(BF16)
        total = jnp.zeros((B, 12 * PP), F32)
        for i in range(4):
            place = iota((PTS, 12 * PP), 1) % (4 * PP) == iota((PTS, 12 * PP), 0) + PP * i
            total = total + exact_dot(lf[:, i, :], jnp.where(place, 1.0, 0.0), TN)
        total = jnp.concatenate([total, jnp.zeros((48 - B, 12 * PP), F32)], axis=0)
        llift[...] = stacked(total, iota((48, 12 * PP), 1) >= 8 * PP)
        place = jnp.where(iota((PTS, 3 * PP), 1) % PP == iota((PTS, 3 * PP), 0), 1.0, 0.0)
        pad = jnp.zeros((PP - PTS, 3 * PP), F32)
        turns = []
        for h in range(3):
            turns += [exact_dot(ro[h], place, TN), pad]
        lrot[...] = stacked(jnp.concatenate(turns, axis=0), iota((3 * PP, 3 * PP), 1) >= 2 * PP)

        lam, mu, rho = mat[0:1, :], mat[1:2, :], mat[2:3, :]
        speed = 0.5 * jnp.sqrt((lam + 2.0 * mu) / rho)
        slip_scale = 1.0 / jnp.sqrt(mu * rho)
        slot_params = jnp.zeros((3 * PP, SLOTS + LANES), F32)
        for i in range(4):
            nx, ny, nz = fn[0, i:i + 1, :], fn[1, i:i + 1, :], fn[2, i:i + 1, :]
            cw = speed * jnp.sqrt(nx * nx + ny * ny + nz * nz)
            rows = [0.5 * nx, 0.5 * ny, 0.5 * nz, cw]
            for j, row in enumerate(rows):
                fcoef[i, j] = spread(row)
            h = ori[i:i + 1, :]
            m0 = jnp.where(h == 0, 1.0, 0.0)
            m1 = jnp.where(h == 1, 1.0, 0.0)
            turn[i, 0] = spread(m0)
            turn[i, 1] = spread(m1)
            rows += [-lam, -2.0 * mu, -mu, -1.0 / rho, slip_scale, m0, m1]
            which = iota((PP, E), 0)
            block = jnp.zeros((PP, E), F32)
            for j, row in enumerate(rows):
                block = jnp.where(which == j, jnp.broadcast_to(row, (PP, E)), block)

            code = nc[i:i + 1, :]
            for j in range(4):
                p1[i, E * j:E * j + E, :] = jnp.where(iota((E, E), 0) + E * j == code, 1.0, 0.0).astype(BF16)
            halo = code - 1024
            number = jnp.zeros_like(halo)
            for m in range(1, 8):
                number = number + jnp.where(halo >= 28 * m, 1, 0)
            fault = code - 1248
            spot = jnp.where(fault >= 0, fault + SLOTS, jnp.where(halo >= 0, halo + 4 * number, -1))
            hot = jnp.where(iota((SLOTS + LANES, E), 0) == spot, 1.0, 0.0).astype(BF16)
            p2[i] = hot
            hi, rest = halves(block)
            mid, lo = halves(rest)
            left = jnp.concatenate([hi, mid, lo], axis=0).astype(BF16)
            slot_params = slot_params + lax.dot_general(
                left, hot, (((1,), (1,)), ((), ())), preferred_element_type=F32
            )
        slot_params = slot_params[0:PP] + slot_params[PP:2 * PP] + slot_params[2 * PP:3 * PP]
        for j in range(11):
            scoef[j] = jnp.broadcast_to(slot_params[j:j + 1, :], (8, SLOTS + LANES))

        fdip[...] = jnp.zeros_like(fdip)
        fdip[0:2, 0:FAULTS] = dip[...]
        polar, azimuth = fdip[0:1, :], fdip[1:2, :]
        fric[0] = jnp.broadcast_to(jnp.sin(polar) * jnp.cos(azimuth), (PP, LANES))
        fric[1] = jnp.broadcast_to(jnp.sin(polar) * jnp.sin(azimuth), (PP, LANES))
        fric[2] = jnp.broadcast_to(jnp.cos(polar), (PP, LANES))
        fric[3] = jnp.ones((PP, LANES), F32)
        fric[3, 0:PTS, 0:FAULTS] = coh[...]

    def split_modes(x):
        hi, lo = halves(x)
        return jnp.concatenate([hi, lo, hi, jnp.zeros((8, E), F32)], axis=0).astype(BF16)

    def sum_elastic(store):
        def body(rb, carry):
            def get(q, d):
                return R[q, pl.ds(pl.multiple_of(BP * d + 8 * rb, 8), 8), :]

            g = [[coef[3 * d + c] for c in range(3)] for d in range(3)]
            m = [coef[9 + j] for j in range(4)]
            grad = {}
            for i in range(3):
                v = [get(6 + i, d) for d in range(3)]
                for c in range(3):
                    grad[i, c] = v[0] * g[0][c] + v[1] * g[1][c] + v[2] * g[2][c]
            pressure = m[0] * (grad[0, 0] + grad[1, 1] + grad[2, 2])
            res = [
                pressure + m[1] * grad[0, 0],
                pressure + m[1] * grad[1, 1],
                pressure + m[1] * grad[2, 2],
                m[2] * (grad[0, 1] + grad[1, 0]),
                m[2] * (grad[1, 2] + grad[2, 1]),
                m[2] * (grad[0, 2] + grad[2, 0]),
            ]
            for kinds in ((0, 3, 5), (3, 1, 4), (5, 4, 2)):
                force = None
                for c, q in enumerate(kinds):
                    for d in range(3):
                        term = get(q, d) * g[d][c]
                        force = term if force is None else force + term
                res.append(m[3] * force)
            store(pl.ds(pl.multiple_of(8 * rb, 8), 8), res)
            return carry

        lax.fori_loop(0, BP // 8, body, 0, unroll=True)

    def send(step, k):
        return pltpu.make_async_remote_copy(
            src_ref=sendb.at[step, pl.ds(32 * k, 32)],
            dst_ref=recvb.at[step, pl.ds(32 * k, 32)],
            send_sem=send_sem.at[step, k],
            recv_sem=recv_sem.at[step, k],
            device_id=(me + OFFSETS[k], sub),
            device_id_type=MESH,
        )

    def send_fault(step):
        return pltpu.make_async_remote_copy(
            src_ref=sendf.at[step],
            dst_ref=recvf.at[step],
            send_sem=fsend_sem.at[step],
            recv_sem=frecv_sem.at[step],
            device_id=(me, partner),
            device_id_type=MESH,
        )

    def shifted(x, by):
        return jnp.concatenate(
            [pltpu.roll(x[:, LANES * t:LANES * t + LANES], by % LANES, 1) for t in range(SLOTS // LANES)], axis=1
        )

    in_block = iota((8, SLOTS), 1) & 31
    last_row = iota((8, SLOTS), 0) == 7

    def turned(x, first, second):
        r = fast_dot(lrot[...], jnp.concatenate([x[0], x[1], x[0]], axis=0))
        return jnp.where(first, r[0:PP], jnp.where(second, r[PP:2 * PP], r[2 * PP:3 * PP]))

    def slot_coefs(lanes):
        def double(j):
            return jnp.concatenate([scoef[j, :, lanes], scoef[j, :, lanes]], axis=0)

        return [double(j) for j in range(11)]

    def outer_flux(far, c):
        flux = elastic_rows(far, c[0:3], c[4:8])
        return [flux[q] - c[3] * far[q] for q in range(Q)]

    def stacked_rows(flux):
        parts = [halves(f) for f in flux]
        return jnp.concatenate([p[0] for p in parts] + [p[1] for p in parts], axis=0).astype(BF16)

    def update(step):
        def forces(rows, sigma):
            g = [[coef[3 * d + c] for c in range(3)] for d in range(3)]
            for c, kinds in enumerate(((0, 3, 5), (3, 1, 4), (5, 4, 2))):
                for d in range(3):
                    pull[3 * c + d, rows, :] = (
                        sigma[kinds[0]] * g[d][0] + sigma[kinds[1]] * g[d][1] + sigma[kinds[2]] * g[d][2]
                    )

        def first(rb, carry):
            rows = pl.ds(pl.multiple_of(8 * rb, 8), 8)
            forces(rows, [state[q, rows, :] for q in range(6)])
            return carry

        lax.fori_loop(0, BP // 8, first, 0, unroll=True)
        factor = 1.0
        for degree in range(1, DEGREES + 1):
            for i in range(3):
                x = state[6 + i] if degree == 1 else cur[6 + i]
                R[i] = fast_dot(lpred[...], split_modes(x))
            for c in range(3):
                pieces = []
                for d in range(3):
                    hi, lo = halves(pull[3 * c + d])
                    pieces += [hi, lo, hi]
                pieces = jnp.concatenate(pieces + [jnp.zeros((24, E), F32)], axis=0).astype(BF16)
                drive[c] = fast_dot(lforce[...], pieces)
            factor = factor / (degree + 1)

            def body(rb, carry, factor=factor, degree=degree):
                rows = pl.ds(pl.multiple_of(8 * rb, 8), 8)
                g = [[coef[3 * d + c] for c in range(3)] for d in range(3)]
                m = [coef[9 + j] for j in range(4)]
                grad = {}
                for i in range(3):
                    v = [R[i, pl.ds(pl.multiple_of(BP * d + 8 * rb, 8), 8), :] for d in range(3)]
                    for c in range(3):
                        grad[i, c] = v[0] * g[0][c] + v[1] * g[1][c] + v[2] * g[2][c]
                pressure = m[0] * (grad[0, 0] + grad[1, 1] + grad[2, 2])
                res = [
                    pressure + m[1] * grad[0, 0],
                    pressure + m[1] * grad[1, 1],
                    pressure + m[1] * grad[2, 2],
                    m[2] * (grad[0, 1] + grad[1, 0]),
                    m[2] * (grad[1, 2] + grad[2, 1]),
                    m[2] * (grad[0, 2] + grad[2, 0]),
                ]
                res += [m[3] * drive[c, rows, :] for c in range(3)]
                base = state if degree == 1 else integ
                for q in range(Q):
                    integ[q, rows, :] = base[q, rows, :] + factor * res[q]
                if degree < DEGREES:
                    for i in range(3):
                        cur[6 + i, rows, :] = res[6 + i]
                    forces(rows, res[0:6])
                return carry

            lax.fori_loop(0, BP // 8, body, 0, unroll=True)

        for q in range(Q):
            t = fast_dot(lprj[...], split_modes(integ[q]))
            tr[q] = t
            hi, lo = both(t)
            for i in range(4):
                ths[PP * q:PP * q + PP, E * i:E * i + E] = hi[PP * i:PP * i + PP]
                ths[ROWS + PP * q:ROWS + PP * q + PP, E * i:E * i + E] = lo[PP * i:PP * i + PP]

        picked = fast_dot(ths[...], sp[...])
        picked = picked[0:ROWS] + picked[ROWS:2 * ROWS]
        tail = picked[128 + 8:ROWS]
        tiles = []
        for t in range(16):
            x = picked[8 * t:8 * t + 8]
            if t % 2 == 1:
                x = jnp.where(last_row, jnp.broadcast_to(picked[128 + t // 2:129 + t // 2], (8, SLOTS)), x)
            if t < 7:
                x = jnp.where(in_block >= 28, shifted(tail, 28 - 4 * t), x)
            tiles.append(x)
        sendb[step] = jnp.transpose(jnp.concatenate(tiles, axis=0))

        if step == 0:
            pl.semaphore_wait(barrier, 1 + jnp.minimum(me, 4) + jnp.minimum(n_dom - 1 - me, 4))

        far_first = (3, 7, 2, 6, 1, 5, 0, 4)

        @pl.when(inside)
        def _():
            for k in far_first:
                send(step, k).start()

        @pl.when(jnp.logical_not(inside))
        def _():
            for k in far_first:
                dst = me + OFFSETS[k]

                @pl.when((dst >= 0) & (dst < n_dom))
                def _():
                    send(step, k).start()

        if step == 0:
            setup_fault()

        picked = fast_dot(ths[...], spf[...])
        picked = picked[0:ROWS] + picked[ROWS:2 * ROWS]
        sgf[...] = picked
        sendf[step] = (
            picked[0:3 * PP]
            + pltpu.roll(picked[3 * PP:6 * PP], FAULTS, 1)
            + pltpu.roll(picked[6 * PP:9 * PP], 2 * FAULTS, 1)
        )
        send_fault(step).start()

        if step == 0:
            setup_rest()

        def own_face(i, c):
            g = fast_dot(ths[...], p1[i]).astype(BF16)
            m0, m1 = turn[i, 0] > 0.5, turn[i, 1] > 0.5
            for q in range(Q):
                hi = g[PP * q:PP * q + PP]
                lo = g[ROWS + PP * q:ROWS + PP * q + PP]
                r = fast_dot(lrot[...], jnp.concatenate([hi, lo, hi], axis=0))
                for half in range(2):
                    a = 8 * half
                    rt[q, pl.ds(pl.multiple_of(PP * i + a, 8), 8), :] = jnp.where(
                        m0, r[a:a + 8], jnp.where(m1, r[PP + a:PP + a + 8], r[2 * PP + a:2 * PP + a + 8])
                    )
            m = [coef[9 + j] for j in range(4)]
            n = [fcoef[i, j] for j in range(3)]
            cw = fcoef[i, 3]
            for half in range(2):
                rows = pl.ds(pl.multiple_of(PP * i + 8 * half, 8), 8)
                own = [tr[q, rows, :] for q in range(Q)]
                far = [rt[q, rows, :] for q in range(Q)]
                res = elastic_rows([x + y for x, y in zip(own, far)], n, m)
                for q in range(Q):
                    fx[q, rows, :] = res[q] + cw * (own[q] - far[q])
            return c

        lax.fori_loop(0, 4, own_face, 0, unroll=True)

        for q in range(Q):
            R[q] = fast_dot(lvol[...], split_modes(integ[q]))

        def store_volume(rows, res):
            for q in range(Q):
                cur[q, rows, :] = state[q, rows, :] + res[q]

        sum_elastic(store_volume)

        send_fault(step).wait_recv()
        c = slot_coefs(slice(SLOTS, SLOTS + LANES))
        first, second = c[9] > 0.5, c[10] > 0.5
        came = recvf[step]
        came = [came, pltpu.roll(came, LANES - FAULTS, 1), pltpu.roll(came, LANES - 2 * FAULTS, 1)]
        came = jnp.concatenate(came, axis=0)
        far = [turned(both(came[PP * q:PP * q + PP]), first, second) for q in range(Q)]
        flux = outer_flux(far, c)
        u = (fric[0], fric[1], fric[2])
        mean = [0.5 * (sgf[PP * q:PP * q + PP, :] + far[q]) for q in range(6)]
        force = traction(mean, u)
        along = force[0] * u[0] + force[1] * u[1] + force[2] * u[2]
        tangent = [force[a] - along * u[a] for a in range(3)]
        strength = fric[3] + FRICTION * jnp.maximum(-along, 0.0)
        size = jnp.sqrt(tangent[0] * tangent[0] + tangent[1] * tangent[1] + tangent[2] * tangent[2])
        over = 1.0 - strength / jnp.maximum(size, strength)
        for a in range(3):
            excess = over * tangent[a]
            flux[6 + a] = flux[6 + a] + excess * c[7]
            slipsum[PP * a:PP * a + PP, :] += excess * c[8]
        left = stacked_rows(flux)
        for i in range(4):
            r = fast_dot(left, p2[i, SLOTS:SLOTS + LANES, :])
            for q in range(Q):
                fx[q, PP * i:PP * i + PP, :] += r[PP * q:PP * q + PP] + r[ROWS + PP * q:ROWS + PP * q + PP]

        for q in range(Q):
            hi, lo = both(fx[q])
            lifted = fast_dot(llift[...], jnp.concatenate([hi, lo, hi], axis=0))
            cur[q] = cur[q] - lifted[0:BP]

        for k, o in enumerate(OFFSETS):
            dst = me + o

            @pl.when((dst >= 0) & (dst < n_dom))
            def _():
                send(step, k).wait_send()

        send_fault(step).wait_send()

        for k in (0, 4, 1, 5, 2, 6, 3, 7):
            src = me - OFFSETS[k]

            @pl.when((src >= 0) & (src < n_dom))
            def _():
                send(step, k).wait_recv()

        main = jnp.transpose(recvb[step])
        tail = jnp.zeros((8, SLOTS), F32)
        for t in range(7):
            tail = jnp.where((in_block >> 2) == t, shifted(main[8 * t:8 * t + 8], 4 * t - 28), tail)
        last = jnp.concatenate([main[PP * q + PTS:PP * q + PP] for q in range(8)] + [tail], axis=0)
        c = slot_coefs(slice(0, SLOTS))
        first, second = c[9] > 0.5, c[10] > 0.5
        far = [
            turned(both(main[PP * q:PP * q + PP] if q < 8 else last), first, second) for q in range(Q)
        ]
        left = stacked_rows(outer_flux(far, c))
        for i in range(4):
            hs[i] = fast_dot(left, p2[i, 0:SLOTS, :]).astype(BF16)
        for q in range(Q):
            his = [hs[i, PP * q:PP * q + PP, :] for i in range(4)]
            los = [hs[i, ROWS + PP * q:ROWS + PP * q + PP, :] for i in range(4)]
            lifted = fast_dot(llift[...], jnp.concatenate(his + los + his, axis=0))
            if step < STEPS - 1:
                state[q] = cur[q] - lifted[0:BP]
            else:
                out[q] = cur[q, 0:B, :] - lifted[0:B]

    for step in range(STEPS):
        update(step)

    for a in range(3):
        slip[a] = slipsum[PP * a:PP * a + PTS, 0:FAULTS]


def select_live(live, un, updated, slip, out_hbm, slip_hbm, out, sem):
    copies = [pltpu.make_async_copy(slip, slip_hbm, sem.at[PARTS])]
    copies[0].start()
    alive = jnp.broadcast_to(iota((1, E), 1) < live[0:1, 0:1], (B, E))
    size = Q // PARTS
    for part in range(PARTS):
        for q in range(part * size, part * size + size):
            out[q] = jnp.where(alive, updated[q], un[q])
        rows = pl.ds(part * size, size)
        copies.append(pltpu.make_async_copy(out.at[rows], out_hbm.at[rows], sem.at[part]))
        copies[-1].start()
    for copy in copies:
        copy.wait()


def on_device(n_dom, *args):
    (un, gr, fn, mat, live, nc, ori, sf, ff, dip, coh, st, pj, lf, ro) = args
    fn = jnp.transpose(fn, (1, 0, 2))
    pj = jnp.transpose(pj, (2, 0, 1))
    lf = jnp.transpose(lf, (1, 0, 2))
    args = (un, gr, fn, mat, nc, ori, sf.reshape(1, -1), ff.reshape(1, -1), dip, coh, st, pj, lf, ro)
    vmem = pl.BlockSpec(memory_space=pltpu.VMEM)
    args = [pltpu.with_memory_space_constraint(a, pltpu.HBM) for a in args]

    def f32(*shape):
        return pltpu.VMEM(shape, F32)

    def b16(*shape):
        return pltpu.VMEM(shape, BF16)

    updated, slip = pl.pallas_call(
        functools.partial(kernel, n_dom),
        out_shape=(
            jax.ShapeDtypeStruct((Q, B, E), F32),
            jax.ShapeDtypeStruct((3, PTS, FAULTS), F32),
        ),
        in_specs=[pl.BlockSpec(memory_space=pltpu.HBM)] * len(args),
        out_specs=(vmem, vmem),
        scratch_shapes=[pltpu.VMEM(a.shape, a.dtype) for a in args] + [
            f32(Q, BP, E),
            f32(Q, BP, E),
            f32(Q, BP, E),
            f32(Q, 128, E),
            f32(Q, 4 * PP, E),
            b16(2 * ROWS, 4 * E),
            f32(Q, 4 * PP, E),
            f32(Q, 4 * PP, E),
            b16(4, 4 * E, E),
            b16(4, SLOTS + LANES, E),
            b16(4 * E, SLOTS),
            b16(4 * E, LANES),
            b16(4, 2 * ROWS, E),
            f32(Q, BP, E),
            f32(3, 48, E),
            f32(128, 128),
            f32(4 * PP, 128),
            b16(48, 384),
            b16(128, 128),
            b16(128, 128),
            b16(4 * PP, 128),
            b16(48, 12 * PP),
            b16(3 * PP, 3 * PP),
            f32(13, 8, E),
            f32(4, 4, 8, E),
            f32(4, 2, 8, E),
            f32(11, 8, SLOTS + LANES),
            pltpu.VMEM((8, LANES), jnp.int32),
            f32(8, LANES),
            f32(4, PP, LANES),
            f32(3 * PP, LANES),
            f32(STEPS, SLOTS, LANES),
            f32(STEPS, SLOTS, LANES),
            f32(ROWS, LANES),
            f32(STEPS, 3 * PP, LANES),
            f32(STEPS, 3 * PP, LANES),
            pltpu.SemaphoreType.DMA((len(args),)),
            pltpu.SemaphoreType.DMA((STEPS, 8)),
            pltpu.SemaphoreType.DMA((STEPS, 8)),
            pltpu.SemaphoreType.DMA((STEPS,)),
            pltpu.SemaphoreType.DMA((STEPS,)),
        ],
        compiler_params=pltpu.CompilerParams(
            collective_id=0, has_side_effects=True, vmem_limit_bytes=40 * 1024 * 1024
        ),
        name="ader_updates",
    )(*args)
    live = lax.pad(live, jnp.int32(0), ((0, LANES - 1, 0),)).reshape(1, LANES)
    hbm = pl.BlockSpec(memory_space=pl.ANY)
    return pl.pallas_call(
        select_live,
        out_shape=(
            jax.ShapeDtypeStruct((Q, B, E), F32),
            jax.ShapeDtypeStruct((3, PTS, FAULTS), F32),
        ),
        in_specs=[vmem] * 4,
        out_specs=(hbm, hbm),
        scratch_shapes=[f32(Q, B, E), pltpu.SemaphoreType.DMA((PARTS + 1,))],
        compiler_params=pltpu.CompilerParams(vmem_limit_bytes=4 * 1024 * 1024),
        name="select_live",
    )(live, un, updated, slip)


def solution(mesh):
    split3 = P(None, None, ("dom", "sub"))
    split2 = P(None, ("dom", "sub"))
    split1 = P(("dom", "sub"))
    placed = (
        split3, split3, split3, split2, split1, split2, split2, split1, split1, split2, split2,
        P(), P(), P(), P(),
    )
    return jax.shard_map(
        functools.partial(on_device, mesh.shape["dom"]),
        mesh=mesh,
        in_specs=placed,
        out_specs=(split3, split3),
        check_vma=False,
    )
```
